32 devices in a mesh: along: 8 (over z, x), across: 4 (over y, core).
Axes of the slice: x: 2, y: 2, z: 4, core: 2. Of those that a mesh axis runs over, the one named last changes fastest.
Arguments:
- features: bfloat16 [32768, 256], P(('along', 'across')), may hold values from -6 to 6
- adj_tiles: bfloat16 [256, 4, 128, 128], P(('along', 'across')), may hold values from -0.25 to 0.25
- adj_index: int32 [256, 4], P(('along', 'across')), may hold values from 0 to 11, as said below
- adj_count: int32 [256], P(('along', 'across')), may hold values from 2 to 4, as said below
- bnd_index: int32 [4096], P(('along', 'across')), may hold values from 0 to 1023
- pool_index: int32 [32768], P(('along', 'across')), may hold values from 0 to 15
- w_msg: bfloat16 [256, 256], replicated, may hold values from -0.375 to 0.375
- w_update: bfloat16 [512, 256], replicated, may hold values from -0.25 to 0.25
- w_coarse: bfloat16 [256, 256], replicated, may hold values from -0.375 to 0.375
- cotangent: bfloat16 [32768, 256], P(('along', 'across')), may hold values from -0.3125 to 0.3125
Outputs:
- updated: bfloat16 [32768, 256], P(('along', 'across'))
- weight_grads: float32 [131072], P(('along', 'across'))
The draws below stay inside these ranges and needn't reach their ends.
Inputs may be any that keep to these rules, and one draw needn't show every extreme that they name: `adj_index`: indices 0 to 7 name the partition's own blocks, 8 to 11 the four boundary tiles in the order of the sources. Slot 0 of every block names the block itself. Slots from adj_count on are ignored. Some block has all 4 slots live.
All inputs are finite; a program needn't handle non-finite values.
Results may differ from the reference program's by a relative error of at most 0.0062.
Values may be sent and summed in bfloat16 or wider, within the bound.
A program may use at most 64 MiB of HBM per device.

```python
import jax
import jax.numpy as jnp
from jax import lax

H = 256
TILE = 128
BLK_DEV = 8
KT = 4
NODE_DEV = 1024
NODES = 32768
NBLK = 256
NCS = 16
N_ALONG = 8
N_ACROSS = 4


def draw_adj_index(key, part):
    first_key, second_key = jax.random.split(jax.random.fold_in(key, 11))
    block_ids = jnp.arange(NBLK, dtype=jnp.int32)
    local_block = block_ids % BLK_DEV
    owner = block_ids // BLK_DEV
    turn = jax.random.randint(first_key, (NBLK // BLK_DEV,), 0, 4, dtype=jnp.int32)
    side = BLK_DEV + (local_block + turn[owner]) % 4
    others = jax.random.randint(second_key, (NBLK, KT - 2), 0, BLK_DEV + 4, dtype=jnp.int32)
    return jnp.concatenate([local_block[:, None], side[:, None], others], axis=1).astype(jnp.int32)


def draw_adj_count(key, part):
    first_key, second_key = jax.random.split(jax.random.fold_in(key, 23))
    level = jax.random.randint(first_key, (NBLK // BLK_DEV,), 2, KT + 1, dtype=jnp.int32)
    jitter = jax.random.randint(second_key, (NBLK,), -1, 2, dtype=jnp.int32)
    owner = jnp.arange(NBLK, dtype=jnp.int32) // BLK_DEV
    counts = jnp.clip(level[owner] + jitter, 2, KT)
    return counts.at[0].set(KT).astype(jnp.int32)


def with_ends(values, rng, least, high):
    extent = values.shape
    spot = [jax.random.randint(jax.random.fold_in(rng, axis), (), 0, extent[axis]) for axis in range(len(extent))]
    values = values.at[tuple(spot)].set(least)
    longest = extent.index(max(extent))
    spot[longest] = (spot[longest] + 1) % extent[longest]
    return values.at[tuple(spot)].set(high)


def strengthened(values, key, source, target, parts, factor):
    owner, partner = [(jnp.arange(values.shape[position]) // (values.shape[position] // parts)).reshape([-1 if axis == position else 1 for axis in range(values.ndim)]) for position in (source, target)]
    chosen = jax.random.permutation(key, parts)[partner]
    strong = (owner == chosen) | (owner == (partner + parts // 2) % parts)
    return jnp.where(strong, factor * values, values)


def block_scale(own_key, dims, shards, least, high):
    def one(dim, parts):
        steps = jax.random.uniform(jax.random.fold_in(jax.random.fold_in(own_key, 6), dim), (parts,), jnp.float32, least / len(shards), high / len(shards))
        return jnp.repeat(jnp.exp(steps), dims[dim] // parts).reshape((-1,) + (1,) * (len(dims) - dim - 1))

    loudness = one(*shards[0])
    for cut in shards[1:]:
        loudness = loudness * one(*cut)
    return loudness


def scatter_about(stream_key, dims, deviation, bound, shards=(), kind=jnp.bfloat16):
    values = deviation * jax.random.normal(stream_key, dims, jnp.float32)
    if shards:
        values = values * block_scale(stream_key, dims, shards, -0.22, 0.18)
    return jnp.clip(values, -bound, bound).astype(kind)


def bell_draw_with(stream_key, extent, width, bound, shards, heavy, kind=jnp.bfloat16):
    drawn = width * jax.random.normal(stream_key, extent, jnp.float32)
    if shards:
        drawn = drawn * block_scale(stream_key, extent, shards, -0.22, 0.18)
    return jnp.clip(strengthened(drawn, jax.random.fold_in(stream_key, 3), *heavy), -bound, bound).astype(kind)


def setup_inputs(seed: int = 0) -> dict:
    key_of = jax.random.split(jax.random.key(seed), 11)
    return {
        "features": scatter_about(key_of[0], (NODES, H), 1.0, 6.0, ((0, 32),)),
        "adj_tiles": scatter_about(key_of[1], (NBLK, KT, TILE, TILE), (KT * TILE) ** -0.5, 0.25, ((0, 32),)),
        "adj_index": draw_adj_index(jax.random.fold_in(key_of[10], 71), 0),
        "adj_count": draw_adj_count(jax.random.fold_in(key_of[10], 71), 0),
        "bnd_index": with_ends(jax.random.randint(key_of[4], (N_ALONG * N_ACROSS * TILE,), 0, NODE_DEV), jax.random.fold_in(key_of[4], 1), 0, NODE_DEV - 1).astype(jnp.int32),
        "pool_index": with_ends(jax.random.randint(key_of[5], (NODES,), 0, NCS), jax.random.fold_in(key_of[5], 1), 0, NCS - 1).astype(jnp.int32),
        "w_msg": scatter_about(key_of[6], (H, H), H ** -0.5, 0.375),
        "w_update": scatter_about(key_of[7], (2 * H, H), (2 * H) ** -0.5, 0.25),
        "w_coarse": scatter_about(key_of[8], (H, H), H ** -0.5, 0.375),
        "cotangent": bell_draw_with(key_of[9], (NODES, H), (2.0 * NODES ** -0.5), 0.3125, ((0, 32),), (0, 1, 32, 2.75)),
    }


eps = 1e-05

def normalize(values):
    center = values - lax.optimization_barrier(jnp.mean(values, axis=-1, keepdims=True))
    inverse = lax.rsqrt(lax.optimization_barrier(jnp.mean(center * center, axis=-1, keepdims=True)) + eps)
    return (center * inverse, inverse)

def silu_slope(values):
    logistic = jax.nn.sigmoid(values)
    return logistic * (1.0 + values * (1.0 - logistic))

def pick_rows(matrix_rows, row_index):
    return matrix_rows[row_index]

def reference(features, adj_tiles, adj_index, adj_count, bnd_index, pool_index, w_msg, w_update, w_coarse, cotangent):
    devices = N_ALONG * N_ACROSS
    node_dev = BLK_DEV * TILE
    inputs = features.astype(jnp.float32)
    normed, _ = normalize(inputs)
    scaled = normed.astype(jnp.bfloat16)
    local_rows = scaled.reshape(devices, node_dev, H)
    rim_index = bnd_index.reshape(devices, TILE)
    rim_rows = jax.vmap(pick_rows)(local_rows, rim_index)
    rim_grid = rim_rows.reshape(N_ALONG, N_ACROSS, TILE, H)
    padded = jnp.pad(rim_grid, ((1, 1), (1, 1), (0, 0), (0, 0)))
    halo_tiles = jnp.stack([padded[:-2, 1:-1], padded[2:, 1:-1], padded[1:-1, :-2], padded[1:-1, 2:]], axis=2)
    halo_tiles = halo_tiles.reshape(devices, 4, TILE, H)
    sources = jnp.concatenate([local_rows.reshape(devices, BLK_DEV, TILE, H), halo_tiles], axis=1)
    messages = jnp.dot(sources.reshape(-1, H), w_msg, preferred_element_type=jnp.float32)
    messages = messages.astype(jnp.bfloat16).reshape(sources.shape)
    live_slots = jnp.arange(KT)[None, :] < adj_count[:, None]
    tiles_dev = adj_tiles.reshape(devices, BLK_DEV, KT, TILE, TILE)
    index_dev = adj_index.reshape(devices, BLK_DEV, KT)
    live_dev = live_slots.reshape(devices, BLK_DEV, KT)

    def aggregate(operands):
        tile_set, index_set, live_set, message_set, source_set = operands
        weights = jnp.where(live_set[:, :, None, None], tile_set.astype(jnp.float32), jnp.zeros((), jnp.float32))
        first = jnp.einsum('bkij,bkjh->bih', weights, message_set[index_set].astype(jnp.float32), precision=lax.Precision.HIGHEST)
        second = jnp.einsum('bkij,bkjh->bih', weights, source_set[index_set].astype(jnp.float32), precision=lax.Precision.HIGHEST)
        return (first.astype(jnp.bfloat16), second.astype(jnp.bfloat16))
    aggregated, summed_scaled = lax.map(aggregate, (tiles_dev, index_dev, live_dev, messages, sources))
    aggregated = aggregated.reshape(NODES, H)
    summed_scaled = summed_scaled.reshape(NODES, H)
    joined = jnp.concatenate([scaled, aggregated], axis=1)
    update_pre = jnp.dot(joined, w_update, preferred_element_type=jnp.float32)
    hidden_one = inputs + jax.nn.silu(update_pre)
    segment_ids = (jnp.arange(NODES) // node_dev // N_ACROSS * NCS).astype(jnp.int32) + pool_index.astype(jnp.int32)
    pooled = jax.ops.segment_sum(hidden_one, segment_ids, num_segments=N_ALONG * NCS)
    coarse_norm, inverse = normalize(pooled)
    coarse = coarse_norm.astype(jnp.bfloat16)
    coarse_pre = jnp.dot(coarse, w_coarse, preferred_element_type=jnp.float32)
    coarse_out = jax.nn.silu(coarse_pre).astype(jnp.bfloat16)
    hidden_two = hidden_one + coarse_out[segment_ids].astype(jnp.float32)
    cot_float = cotangent.astype(jnp.float32)
    coarse_cot = jax.ops.segment_sum(cot_float, segment_ids, num_segments=N_ALONG * NCS)
    coarse_delta = (coarse_cot * silu_slope(coarse_pre)).astype(jnp.bfloat16)
    coarse_grad = jnp.dot(coarse.T, coarse_delta, preferred_element_type=jnp.float32)
    coarse_back = jnp.dot(coarse_delta, w_coarse.T, preferred_element_type=jnp.float32)
    mean_one = lax.optimization_barrier(jnp.mean(coarse_back, axis=-1, keepdims=True))
    mean_two = lax.optimization_barrier(jnp.mean(coarse_back * coarse_norm, axis=-1, keepdims=True))
    pooled_delta = inverse * (coarse_back - mean_one - coarse_norm * mean_two)
    hidden_delta = cot_float + pooled_delta[segment_ids]
    update_delta = (hidden_delta * silu_slope(update_pre)).astype(jnp.bfloat16)
    aggregated_delta = jnp.dot(update_delta, w_update[H:].T, preferred_element_type=jnp.float32).astype(jnp.bfloat16)
    message_grad = jnp.dot(summed_scaled.T, aggregated_delta, preferred_element_type=jnp.float32)
    weight_grads = jnp.concatenate([message_grad.reshape(-1), coarse_grad.reshape(-1)])
    return (hidden_two.astype(jnp.bfloat16), weight_grads)
```

```python
import functools

import jax
import jax.numpy as jnp
from jax import lax
from jax.experimental import pallas as pl
from jax.experimental.pallas import tpu as pltpu
from jax.sharding import PartitionSpec as P

NC_DEV = 4


eps = 1e-05


def extended(block, sides, width):
    for axis, dim in sides:
        count = lax.axis_size(axis)
        forward = [(i, i + 1) for i in range(count - 1)]
        backward = [(target, source) for source, target in forward]
        low = lax.ppermute(
            lax.slice_in_dim(block, block.shape[dim] - width, None, axis=dim), axis, forward
        )
        high = lax.ppermute(lax.slice_in_dim(block, 0, width, axis=dim), axis, backward)
        block = jnp.concatenate([low, block, high], axis=dim)
    return block


def normalize(values):
    center = values - jnp.mean(values, axis=-1, keepdims=True)
    inverse = lax.rsqrt(jnp.mean(center * center, axis=-1, keepdims=True) + eps)
    return (center * inverse, inverse)


def silu_slope(values):
    logistic = jax.nn.sigmoid(values)
    return logistic * (1.0 + values * (1.0 - logistic))


def transposed_times(operand, second, precision=None):
    return lax.dot_general(
        operand,
        second,
        (((0,), (0,)), ((), ())),
        precision=precision,
        preferred_element_type=jnp.float32,
    )


def times_transposed(operand, second):
    return lax.dot_general(
        operand, second, (((1,), (1,)), ((), ())), preferred_element_type=jnp.float32
    )


def coarse_forward(pooled, w_coarse):
    coarse_norm, inverse = normalize(pooled)
    coarse = coarse_norm.astype(jnp.bfloat16)
    coarse_pre = jnp.dot(coarse, w_coarse, preferred_element_type=jnp.float32)
    return (coarse_norm, inverse, coarse, coarse_pre, jax.nn.silu(coarse_pre).astype(jnp.bfloat16))


def coarse_backward(coarse_cot, coarse_norm, inverse, coarse_pre, w_coarse):
    coarse_delta = (coarse_cot * silu_slope(coarse_pre)).astype(jnp.bfloat16)
    coarse_back = times_transposed(coarse_delta, w_coarse)
    mean_one = jnp.mean(coarse_back, axis=-1, keepdims=True)
    mean_two = jnp.mean(coarse_back * coarse_norm, axis=-1, keepdims=True)
    return (coarse_delta, inverse * (coarse_back - mean_one - coarse_norm * mean_two))


def plain_layer(
    features,
    adj_tiles,
    adj_index,
    adj_count,
    bnd_index,
    pool_index,
    w_msg,
    w_update,
    w_coarse,
    cotangent,
):
    feature_count = features.shape[1]
    blocks = adj_tiles.shape[0]
    slot_count = adj_tiles.shape[1]
    tile_rows = adj_tiles.shape[2]
    inputs = features.astype(jnp.float32)
    normed, _ = normalize(inputs)
    scaled = normed.astype(jnp.bfloat16)
    rim_rows = scaled[bnd_index]
    padded = extended(rim_rows[None, None], (("along", 0), ("across", 1)), 1)
    halo_tiles = jnp.stack([padded[0, 1], padded[2, 1], padded[1, 0], padded[1, 2]])
    sources = jnp.concatenate(
        [scaled.reshape(blocks, tile_rows, feature_count), halo_tiles], axis=0
    )
    messages = jnp.dot(
        sources.reshape(-1, feature_count), w_msg, preferred_element_type=jnp.float32
    )
    messages = messages.astype(jnp.bfloat16).reshape(sources.shape)
    live_slots = jnp.arange(slot_count)[None, :] < adj_count[:, None]
    masked_tiles = jnp.where(live_slots[:, :, None, None], adj_tiles, jnp.zeros((), jnp.bfloat16))
    aggregated = jnp.einsum(
        "bkij,bkjh->bih", masked_tiles, messages[adj_index], preferred_element_type=jnp.float32
    )
    aggregated = aggregated.astype(jnp.bfloat16).reshape(-1, feature_count)
    summed_scaled = jnp.einsum(
        "bkij,bkjh->bih", masked_tiles, sources[adj_index], preferred_element_type=jnp.float32
    )
    summed_scaled = summed_scaled.astype(jnp.bfloat16).reshape(-1, feature_count)
    w_first = w_update[:feature_count]
    w_second = w_update[feature_count:]
    update_pre = jnp.dot(scaled, w_first, preferred_element_type=jnp.float32) + jnp.dot(
        aggregated, w_second, preferred_element_type=jnp.float32
    )
    hidden_one = inputs + jax.nn.silu(update_pre)
    coarse_count = NC_DEV * lax.axis_size("across")
    assign_float = (pool_index[:, None] == jnp.arange(coarse_count)[None, :]).astype(jnp.float32)
    assign_bits = assign_float.astype(jnp.bfloat16)
    pooled_part = transposed_times(assign_float, hidden_one, lax.Precision.HIGHEST)
    cot_part = transposed_times(assign_bits, cotangent)
    pooled, coarse_cot = lax.psum((pooled_part, cot_part), "across")
    coarse_norm, inverse, coarse, coarse_pre, coarse_out = coarse_forward(pooled, w_coarse)
    hidden_two = hidden_one + jnp.dot(assign_bits, coarse_out, preferred_element_type=jnp.float32)
    coarse_delta, pooled_delta = coarse_backward(
        coarse_cot, coarse_norm, inverse, coarse_pre, w_coarse
    )
    start = lax.axis_index("across") * NC_DEV
    own_coarse = lax.dynamic_slice_in_dim(coarse, start, NC_DEV, 0)
    own_coarse_delta = lax.dynamic_slice_in_dim(coarse_delta, start, NC_DEV, 0)
    coarse_grad = transposed_times(own_coarse, own_coarse_delta)
    hidden_delta = cotangent.astype(jnp.float32) + jnp.dot(
        assign_float,
        pooled_delta,
        precision=lax.Precision.HIGHEST,
        preferred_element_type=jnp.float32,
    )
    update_delta = (hidden_delta * silu_slope(update_pre)).astype(jnp.bfloat16)
    aggregated_delta = times_transposed(update_delta, w_second).astype(jnp.bfloat16)
    message_grad = transposed_times(summed_scaled, aggregated_delta)
    grad_terms = jnp.concatenate([message_grad.reshape(-1), coarse_grad.reshape(-1)])
    partial_grads = lax.psum_scatter(grad_terms, "along", scatter_dimension=0, tiled=True)
    weight_grads = lax.psum_scatter(partial_grads, "across", scatter_dimension=0, tiled=True)
    return (hidden_two.astype(jnp.bfloat16), weight_grads)


MESH = pl.DeviceIdType.MESH
f32 = jnp.float32
bf16 = jnp.bfloat16


def split(values):
    high = values.astype(bf16)
    return high, (values - high.astype(f32)).astype(bf16)


def dot(first, second):
    return jnp.dot(first, second, preferred_element_type=f32)


def sigmoid(values):
    return 0.5 * jnp.tanh(0.5 * values) + 0.5


def layer_kernel(
    n_along,
    n_across,
    adj_index,
    adj_count,
    bnd_row,
    pool_row,
    features_hbm,
    adj_hbm,
    w_msg_hbm,
    w_update_hbm,
    w_coarse_hbm,
    cotangent_hbm,
    updated_hbm,
    grads,
    features,
    adj,
    w_msg,
    w_update,
    w_coarse,
    cotangent,
    sources,
    rim,
    w_joined,
    pre,
    hidden,
    slope,
    summed,
    summed_t,
    update_delta,
    updated,
    pool_all,
    cot_all,
    pack,
    pack_all,
    coarse_grad,
    total,
    part,
    part_all,
    second,
    second_all,
    own_chunk,
    in_sem,
    out_sem,
    halo_send,
    halo_recv,
    pool_send,
    pool_recv,
    cot_send,
    cot_recv,
    pack_send,
    pack_recv,
    part_send,
    part_recv,
    second_send,
    second_recv,
):
    a = lax.axis_index("along")
    c = lax.axis_index("across")
    half = n_along // 2
    nodes, width = features.shape
    blocks, slots, tile, _ = adj.shape
    coarse_count = NC_DEV * n_across
    chunk = grads.shape[0]

    loads = [
        pltpu.make_async_copy(source, target, in_sem.at[i])
        for i, (source, target) in enumerate(
            (
                (features_hbm, features),
                (cotangent_hbm, cotangent),
                (w_update_hbm, w_update),
                (w_msg_hbm, w_msg),
                (adj_hbm, adj),
                (w_coarse_hbm, w_coarse),
            )
        )
    ]
    for load in loads:
        load.start()

    barrier = pltpu.get_barrier_semaphore()
    across_peers = [lax.rem(c + d, n_across) for d in range(1, n_across)]
    along_peers = [lax.rem(a + d, n_along) for d in range(1, n_along)]
    for peer in across_peers:
        pl.semaphore_signal(barrier, inc=1, device_id=(a, peer), device_id_type=MESH)
    for peer in along_peers:
        pl.semaphore_signal(barrier, inc=1, device_id=(peer, c), device_id_type=MESH)

    def remote(source, target, send, recv, device):
        return pltpu.make_async_remote_copy(
            src_ref=source,
            dst_ref=target,
            send_sem=send,
            recv_sem=recv,
            device_id=device,
            device_id_type=MESH,
        )

    loads[0].wait()
    for b in range(blocks):
        x = features[b * tile : (b + 1) * tile, :].astype(f32)
        sources[b] = normalize(x)[0].astype(bf16)
    local_rows = sources[0:blocks].reshape(nodes, width)
    rim_pick = (lax.broadcasted_iota(jnp.int32, (nodes, tile), 0) == bnd_row[...]).astype(f32)
    rim[...] = transposed_times(rim_pick.astype(bf16), local_rows).astype(bf16)

    pl.semaphore_wait(barrier, n_across - 1 + n_along - 1)

    sides = (
        (a < n_along - 1, (a + 1, c), a > 0),
        (a > 0, (a - 1, c), a < n_along - 1),
        (c < n_across - 1, (a, c + 1), c > 0),
        (c > 0, (a, c - 1), c < n_across - 1),
    )

    def halo(side, device):
        return remote(
            rim, sources.at[blocks + side], halo_send.at[side], halo_recv.at[side], device
        )

    for side, (has_target, device, has_source) in enumerate(sides):

        @pl.when(has_target)
        def _(side=side, device=device):
            halo(side, device).start()

        @pl.when(jnp.logical_not(has_source))
        def _(side=side):
            sources[blocks + side] = jnp.zeros((tile, width), bf16)

    pool_pick = (
        lax.broadcasted_iota(jnp.int32, (coarse_count, nodes), 0) == pool_row[...]
    ).astype(f32).astype(bf16)
    loads[1].wait()
    cot_all[c] = dot(pool_pick, cotangent[...])
    cot_copies = [
        remote(cot_all.at[c], cot_all.at[c], cot_send.at[d], cot_recv.at[c], (a, peer))
        for d, peer in enumerate(across_peers)
    ]
    for copy in cot_copies:
        copy.start()

    loads[2].wait()
    loads[3].wait()
    w_first = w_update[0:width, :]
    w_second = w_update[width : 2 * width, :]
    w_joined[...] = dot(w_msg[...], w_second).astype(bf16)
    for b in range(blocks):
        pre[b * tile : (b + 1) * tile, :] = dot(sources[b], w_first)

    loads[4].wait()
    for side, (has_target, device, has_source) in enumerate(sides):

        @pl.when(has_source)
        def _(side=side):
            halo(side, (a, c)).wait_recv()

    pooled = jnp.zeros((coarse_count, width), f32)
    for b in range(blocks):
        rows = slice(b * tile, (b + 1) * tile)
        gathered = jnp.concatenate([sources[adj_index[b, k]] for k in range(slots)], axis=0)
        weights = jnp.concatenate(
            [
                adj[b, k]
                * jnp.where(k < adj_count[b], 1.0, 0.0).astype(bf16)
                for k in range(slots)
            ],
            axis=1,
        )
        block_sum = dot(weights, gathered).astype(bf16)
        summed[rows, :] = block_sum
        v = pre[rows, :] + dot(block_sum, w_joined[...])
        s = sigmoid(v)
        slope[rows, :] = s * (1.0 + v * (1.0 - s))
        h = features[rows, :].astype(f32) + v * s
        hidden[rows, :] = h
        high, low = split(h)
        pick = pool_pick[:, rows]
        pooled += dot(pick, high) + dot(pick, low)
    pool_all[c] = pooled
    pool_copies = [
        remote(pool_all.at[c], pool_all.at[c], pool_send.at[d], pool_recv.at[c], (a, peer))
        for d, peer in enumerate(across_peers)
    ]
    for copy in pool_copies:
        copy.start()

    for b in range(blocks):
        rows = slice(b * tile, (b + 1) * tile)
        summed_t[:, rows] = summed[rows, :].T
    loads[5].wait()

    for peer in across_peers:
        remote(
            cot_all.at[peer], cot_all.at[peer], cot_send.at[0], cot_recv.at[peer], (a, c)
        ).wait_recv()
        remote(
            pool_all.at[peer], pool_all.at[peer], pool_send.at[0], pool_recv.at[peer], (a, c)
        ).wait_recv()
    pooled, coarse_cot = pool_all[0], cot_all[0]
    for i in range(1, n_across):
        pooled, coarse_cot = pooled + pool_all[i], coarse_cot + cot_all[i]

    coarse_norm, inverse = normalize(pooled)
    coarse = coarse_norm.astype(bf16)
    coarse_pre = dot(coarse, w_coarse[...])
    s = sigmoid(coarse_pre)
    coarse_out = (coarse_pre * s).astype(bf16)
    coarse_delta = (coarse_cot * (s * (1.0 + coarse_pre * (1.0 - s)))).astype(bf16)
    pack[0:coarse_count, :] = coarse
    pack[coarse_count : 2 * coarse_count, :] = coarse_delta

    def send_pack(target):
        return remote(pack, pack_all.at[a], pack_send.at[target - half], pack_recv.at[a], (target, c))

    for target in range(half, n_along):

        @pl.when(a != target)
        def _(target=target):
            send_pack(target).start()

    coarse_back = times_transposed(coarse_delta, w_coarse[...])
    mean_one = jnp.mean(coarse_back, axis=-1, keepdims=True)
    mean_two = jnp.mean(coarse_back * coarse_norm, axis=-1, keepdims=True)
    pooled_delta = inverse * (coarse_back - mean_one - coarse_norm * mean_two)
    delta_parts = jnp.concatenate(split(pooled_delta), axis=0)
    twice_pick = jnp.concatenate([pool_pick, pool_pick], axis=0)

    for b in range(blocks):
        rows = slice(b * tile, (b + 1) * tile)
        spread = transposed_times(twice_pick[:, rows], delta_parts)
        hidden_delta = cotangent[rows, :].astype(f32) + spread
        update_delta[rows, :] = (hidden_delta * slope[rows, :]).astype(bf16)
    total[...] = dot(summed_t[...], update_delta[...])

    for i in range(half):
        for j in range(n_across):
            start = (i * n_across + j) * chunk
            part[j, i] = total[start : start + chunk, :].astype(bf16)

    def send_part(i, d, peer):
        return remote(
            part.at[peer, i], part_all.at[c, i], part_send.at[d, i], part_recv.at[c, i], (a, peer)
        )

    for i in reversed(range(half)):
        for d, peer in enumerate(across_peers):
            send_part(i, d, peer).start()

    for b in range(blocks):
        rows = slice(b * tile, (b + 1) * tile)
        spread = transposed_times(pool_pick[:, rows], coarse_out)
        updated[rows, :] = (hidden[rows, :] + spread).astype(bf16)
    store = pltpu.make_async_copy(updated, updated_hbm, out_sem.at[0])
    store.start()

    def send_second(i):
        return remote(
            second.at[i], second_all.at[a], second_send.at[i], second_recv.at[a], (i, c)
        )

    for i in reversed(range(half)):
        start = pl.multiple_of((i * n_across + c) * chunk, chunk)
        chunk_sum = total[pl.ds(start, chunk), :]
        for peer in across_peers:
            remote(
                part.at[peer, i], part_all.at[peer, i], part_send.at[0, i], part_recv.at[peer, i], (a, c)
            ).wait_recv()
            chunk_sum = chunk_sum + part_all[peer, i].astype(f32)

        @pl.when(a == i)
        def _(chunk_sum=chunk_sum):
            own_chunk[...] = chunk_sum

        @pl.when(a != i)
        def _(chunk_sum=chunk_sum, i=i):
            second[i] = chunk_sum.astype(bf16)
            send_second(i).start()

    @pl.when(a < half)
    def _():
        chunk_sum = own_chunk[...]
        for peer in along_peers:
            remote(
                second.at[0], second_all.at[peer], second_send.at[0], second_recv.at[peer], (a, c)
            ).wait_recv()
            chunk_sum = chunk_sum + second_all[peer].astype(f32)
        high, low = split(chunk_sum)
        both = times_transposed(jnp.concatenate([high, low], axis=0), w_second)
        grads[...] = both[0:chunk, :] + both[chunk : 2 * chunk, :]

    @pl.when(a >= half)
    def _():
        pack_all[a] = pack[...]
        for peer in along_peers:
            remote(
                pack, pack_all.at[peer], pack_send.at[0], pack_recv.at[peer], (a, c)
            ).wait_recv()
        rows = n_along * coarse_count
        all_coarse = pack_all[:, 0:coarse_count, :].reshape(rows, width)
        all_delta = pack_all[:, coarse_count : 2 * coarse_count, :].reshape(rows, width)
        coarse_grad[...] = transposed_times(all_coarse, all_delta)
        start = pl.multiple_of(((a - half) * n_across + c) * chunk, chunk)
        grads[...] = coarse_grad[pl.ds(start, chunk), :]

    for side, (has_target, device, has_source) in enumerate(sides):

        @pl.when(has_target)
        def _(side=side, device=device):
            halo(side, device).wait_send()

    for copy in cot_copies + pool_copies:
        copy.wait_send()
    for target in range(half, n_along):

        @pl.when(a != target)
        def _(target=target):
            send_pack(target).wait_send()

    for i in range(half):
        for d, peer in enumerate(across_peers):
            send_part(i, d, peer).wait_send()

        @pl.when(a != i)
        def _(i=i):
            send_second(i).wait_send()

    store.wait()


def fused_layer(
    n_along,
    n_across,
    chunk,
    features,
    adj_tiles,
    adj_index,
    adj_count,
    bnd_index,
    pool_index,
    w_msg,
    w_update,
    w_coarse,
    cotangent,
):
    nodes, width = features.shape
    blocks, slots, tile, _ = adj_tiles.shape
    half = n_along // 2
    coarse_count = NC_DEV * n_across
    vmem = pltpu.VMEM
    dma = pltpu.SemaphoreType.DMA
    smem_spec = pl.BlockSpec(memory_space=pltpu.SMEM)
    vmem_spec = pl.BlockSpec(memory_space=pltpu.VMEM)
    any_spec = pl.BlockSpec(memory_space=pl.ANY)
    updated, grads = pl.pallas_call(
        functools.partial(layer_kernel, n_along, n_across),
        name="mesh_layer",
        out_shape=(
            jax.ShapeDtypeStruct((nodes, width), bf16),
            jax.ShapeDtypeStruct((chunk, width), f32),
        ),
        in_specs=[smem_spec] * 2 + [vmem_spec] * 2 + [any_spec] * 6,
        out_specs=(any_spec, vmem_spec),
        scratch_shapes=[
            vmem((nodes, width), bf16),
            vmem(adj_tiles.shape, bf16),
            vmem(w_msg.shape, bf16),
            vmem(w_update.shape, bf16),
            vmem(w_coarse.shape, bf16),
            vmem((nodes, width), bf16),
            vmem((blocks + 4, tile, width), bf16),
            vmem((tile, width), bf16),
            vmem((width, width), bf16),
            vmem((nodes, width), f32),
            vmem((nodes, width), f32),
            vmem((nodes, width), f32),
            vmem((nodes, width), bf16),
            vmem((width, nodes), bf16),
            vmem((nodes, width), bf16),
            vmem((nodes, width), bf16),
            vmem((n_across, coarse_count, width), f32),
            vmem((n_across, coarse_count, width), f32),
            vmem((2 * coarse_count, width), bf16),
            vmem((n_along, 2 * coarse_count, width), bf16),
            vmem((width, width), f32),
            vmem((width, width), f32),
            vmem((n_across, half, chunk, width), bf16),
            vmem((n_across, half, chunk, width), bf16),
            vmem((half, chunk, width), bf16),
            vmem((n_along, chunk, width), bf16),
            vmem((chunk, width), f32),
            dma((6,)),
            dma((1,)),
            dma((4,)),
            dma((4,)),
            dma((n_across,)),
            dma((n_across,)),
            dma((n_across,)),
            dma((n_across,)),
            dma((half,)),
            dma((n_along,)),
            dma((n_across, half)),
            dma((n_across, half)),
            dma((half,)),
            dma((n_along,)),
        ],
        compiler_params=pltpu.CompilerParams(
            collective_id=0, has_side_effects=True, vmem_limit_bytes=40 * 2**20
        ),
        cost_estimate=pl.CostEstimate(
            flops=2 * nodes * width * (slots * tile + 5 * width),
            bytes_accessed=4 * 2**20,
            transcendentals=nodes * width,
        ),
    )(
        adj_index,
        adj_count,
        bnd_index.reshape(1, tile),
        pool_index.reshape(1, nodes),
        features,
        adj_tiles,
        w_msg,
        w_update,
        w_coarse,
        cotangent,
    )
    return updated, grads.reshape(-1)


def layer(axes, features, adj_tiles, *others):
    n_along, n_across = axes["along"], axes["across"]
    width = features.shape[1]
    chunk = 2 * width // (n_along * n_across)
    if n_along % 2 == 0 and chunk and chunk % 16 == 0:
        return fused_layer(n_along, n_across, chunk, features, adj_tiles, *others)
    return plain_layer(features, adj_tiles, *others)


def solution(mesh):
    return jax.shard_map(
        functools.partial(layer, dict(mesh.shape)),
        mesh=mesh,
        in_specs=(
            P(("along", "across"), None),
            P(("along", "across"), None, None, None),
            P(("along", "across"), None),
            P(("along", "across")),
            P(("along", "across")),
            P(("along", "across")),
            P(),
            P(),
            P(),
            P(("along", "across"), None),
        ),
        out_specs=(P(("along", "across"), None), P(("along", "across"))),
        check_vma=False,
    )
```

```python
import functools

import jax
import jax.numpy as jnp
from jax import lax
from jax.experimental import pallas as pl
from jax.experimental.pallas import tpu as pltpu
from jax.sharding import PartitionSpec as P

NC_DEV = 4


eps = 1e-05


def extended(block, sides, width):
    for axis, dim in sides:
        count = lax.axis_size(axis)
        forward = [(i, i + 1) for i in range(count - 1)]
        backward = [(target, source) for source, target in forward]
        low = lax.ppermute(
            lax.slice_in_dim(block, block.shape[dim] - width, None, axis=dim), axis, forward
        )
        high = lax.ppermute(lax.slice_in_dim(block, 0, width, axis=dim), axis, backward)
        block = jnp.concatenate([low, block, high], axis=dim)
    return block


def normalize(values):
    center = values - jnp.mean(values, axis=-1, keepdims=True)
    inverse = lax.rsqrt(jnp.mean(center * center, axis=-1, keepdims=True) + eps)
    return (center * inverse, inverse)


def silu_slope(values):
    logistic = jax.nn.sigmoid(values)
    return logistic * (1.0 + values * (1.0 - logistic))


def transposed_times(operand, second, precision=None):
    return lax.dot_general(
        operand,
        second,
        (((0,), (0,)), ((), ())),
        precision=precision,
        preferred_element_type=jnp.float32,
    )


def times_transposed(operand, second):
    return lax.dot_general(
        operand, second, (((1,), (1,)), ((), ())), preferred_element_type=jnp.float32
    )


def coarse_forward(pooled, w_coarse):
    coarse_norm, inverse = normalize(pooled)
    coarse = coarse_norm.astype(jnp.bfloat16)
    coarse_pre = jnp.dot(coarse, w_coarse, preferred_element_type=jnp.float32)
    return (coarse_norm, inverse, coarse, coarse_pre, jax.nn.silu(coarse_pre).astype(jnp.bfloat16))


def coarse_backward(coarse_cot, coarse_norm, inverse, coarse_pre, w_coarse):
    coarse_delta = (coarse_cot * silu_slope(coarse_pre)).astype(jnp.bfloat16)
    coarse_back = times_transposed(coarse_delta, w_coarse)
    mean_one = jnp.mean(coarse_back, axis=-1, keepdims=True)
    mean_two = jnp.mean(coarse_back * coarse_norm, axis=-1, keepdims=True)
    return (coarse_delta, inverse * (coarse_back - mean_one - coarse_norm * mean_two))


def plain_layer(
    features,
    adj_tiles,
    adj_index,
    adj_count,
    bnd_index,
    pool_index,
    w_msg,
    w_update,
    w_coarse,
    cotangent,
):
    feature_count = features.shape[1]
    blocks = adj_tiles.shape[0]
    slot_count = adj_tiles.shape[1]
    tile_rows = adj_tiles.shape[2]
    inputs = features.astype(jnp.float32)
    normed, _ = normalize(inputs)
    scaled = normed.astype(jnp.bfloat16)
    rim_rows = scaled[bnd_index]
    padded = extended(rim_rows[None, None], (("along", 0), ("across", 1)), 1)
    halo_tiles = jnp.stack([padded[0, 1], padded[2, 1], padded[1, 0], padded[1, 2]])
    sources = jnp.concatenate(
        [scaled.reshape(blocks, tile_rows, feature_count), halo_tiles], axis=0
    )
    messages = jnp.dot(
        sources.reshape(-1, feature_count), w_msg, preferred_element_type=jnp.float32
    )
    messages = messages.astype(jnp.bfloat16).reshape(sources.shape)
    live_slots = jnp.arange(slot_count)[None, :] < adj_count[:, None]
    masked_tiles = jnp.where(live_slots[:, :, None, None], adj_tiles, jnp.zeros((), jnp.bfloat16))
    aggregated = jnp.einsum(
        "bkij,bkjh->bih", masked_tiles, messages[adj_index], preferred_element_type=jnp.float32
    )
    aggregated = aggregated.astype(jnp.bfloat16).reshape(-1, feature_count)
    summed_scaled = jnp.einsum(
        "bkij,bkjh->bih", masked_tiles, sources[adj_index], preferred_element_type=jnp.float32
    )
    summed_scaled = summed_scaled.astype(jnp.bfloat16).reshape(-1, feature_count)
    w_first = w_update[:feature_count]
    w_second = w_update[feature_count:]
    update_pre = jnp.dot(scaled, w_first, preferred_element_type=jnp.float32) + jnp.dot(
        aggregated, w_second, preferred_element_type=jnp.float32
    )
    hidden_one = inputs + jax.nn.silu(update_pre)
    coarse_count = NC_DEV * lax.axis_size("across")
    assign_float = (pool_index[:, None] == jnp.arange(coarse_count)[None, :]).astype(jnp.float32)
    assign_bits = assign_float.astype(jnp.bfloat16)
    pooled_part = transposed_times(assign_float, hidden_one, lax.Precision.HIGHEST)
    cot_part = transposed_times(assign_bits, cotangent)
    pooled, coarse_cot = lax.psum((pooled_part, cot_part), "across")
    coarse_norm, inverse, coarse, coarse_pre, coarse_out = coarse_forward(pooled, w_coarse)
    hidden_two = hidden_one + jnp.dot(assign_bits, coarse_out, preferred_element_type=jnp.float32)
    coarse_delta, pooled_delta = coarse_backward(
        coarse_cot, coarse_norm, inverse, coarse_pre, w_coarse
    )
    start = lax.axis_index("across") * NC_DEV
    own_coarse = lax.dynamic_slice_in_dim(coarse, start, NC_DEV, 0)
    own_coarse_delta = lax.dynamic_slice_in_dim(coarse_delta, start, NC_DEV, 0)
    coarse_grad = transposed_times(own_coarse, own_coarse_delta)
    hidden_delta = cotangent.astype(jnp.float32) + jnp.dot(
        assign_float,
        pooled_delta,
        precision=lax.Precision.HIGHEST,
        preferred_element_type=jnp.float32,
    )
    update_delta = (hidden_delta * silu_slope(update_pre)).astype(jnp.bfloat16)
    aggregated_delta = times_transposed(update_delta, w_second).astype(jnp.bfloat16)
    message_grad = transposed_times(summed_scaled, aggregated_delta)
    grad_terms = jnp.concatenate([message_grad.reshape(-1), coarse_grad.reshape(-1)])
    partial_grads = lax.psum_scatter(grad_terms, "along", scatter_dimension=0, tiled=True)
    weight_grads = lax.psum_scatter(partial_grads, "across", scatter_dimension=0, tiled=True)
    return (hidden_two.astype(jnp.bfloat16), weight_grads)


MESH = pl.DeviceIdType.MESH
f32 = jnp.float32
bf16 = jnp.bfloat16


def split(values):
    high = values.astype(bf16)
    return high, (values - high.astype(f32)).astype(bf16)


def dot(first, second):
    return jnp.dot(first, second, preferred_element_type=f32)


def sigmoid(values):
    return 0.5 * jnp.tanh(0.5 * values) + 0.5


def layer_kernel(
    n_along,
    n_across,
    index_hbm,
    count_hbm,
    bnd_hbm,
    pool_hbm,
    features_hbm,
    adj_hbm,
    w_msg_hbm,
    w_update_hbm,
    w_coarse_hbm,
    cotangent_hbm,
    updated_hbm,
    grads,
    adj_index,
    adj_count,
    bnd_row,
    pool_row,
    features,
    adj,
    w_msg,
    w_update,
    w_coarse,
    cotangent,
    sources,
    rim,
    w_joined,
    pre,
    hidden,
    slope,
    summed,
    summed_t,
    update_delta,
    updated,
    pool_all,
    cot_all,
    pack,
    pack_all,
    coarse_grad,
    total,
    part,
    part_all,
    second,
    second_all,
    own_chunk,
    in_sem,
    out_sem,
    halo_send,
    halo_recv,
    pool_send,
    pool_recv,
    cot_send,
    cot_recv,
    pack_send,
    pack_recv,
    part_send,
    part_recv,
    second_send,
    second_recv,
):
    a = lax.axis_index("along")
    c = lax.axis_index("across")
    half = n_along // 2
    nodes, width = features.shape
    blocks, slots, tile, _ = adj.shape
    coarse_count = NC_DEV * n_across
    chunk = own_chunk.shape[0]

    def put_grads(values):
        lanes = grads.shape[1]
        parts = width // lanes
        for i in range(parts):
            grads[pl.ds(i, chunk, stride=parts), :] = values[:, i * lanes : (i + 1) * lanes]

    loads = [
        pltpu.make_async_copy(source, target, in_sem.at[i])
        for i, (source, target) in enumerate(
            (
                (features_hbm, features),
                (bnd_hbm, bnd_row),
                (pool_hbm, pool_row),
                (cotangent_hbm, cotangent),
                (w_update_hbm, w_update),
                (w_msg_hbm, w_msg),
                (index_hbm, adj_index),
                (count_hbm, adj_count),
                (adj_hbm, adj),
                (w_coarse_hbm, w_coarse),
            )
        )
    ]
    for load in loads:
        load.start()

    barrier = pltpu.get_barrier_semaphore()
    across_peers = [lax.rem(c + d, n_across) for d in range(1, n_across)]
    along_peers = [lax.rem(a + d, n_along) for d in range(1, n_along)]
    for peer in across_peers:
        pl.semaphore_signal(barrier, inc=1, device_id=(a, peer), device_id_type=MESH)
    for peer in along_peers:
        pl.semaphore_signal(barrier, inc=1, device_id=(peer, c), device_id_type=MESH)

    def remote(source, target, send, recv, device):
        return pltpu.make_async_remote_copy(
            src_ref=source,
            dst_ref=target,
            send_sem=send,
            recv_sem=recv,
            device_id=device,
            device_id_type=MESH,
        )

    loads[0].wait()
    for b in range(blocks):
        x = features[b * tile : (b + 1) * tile, :].astype(f32)
        sources[b] = normalize(x)[0].astype(bf16)
    local_rows = sources[0:blocks].reshape(nodes, width)
    loads[1].wait()
    rim_pick = (lax.broadcasted_iota(jnp.int32, (nodes, tile), 0) == bnd_row[...]).astype(f32)
    rim[...] = transposed_times(rim_pick.astype(bf16), local_rows).astype(bf16)

    pl.semaphore_wait(barrier, n_across - 1 + n_along - 1)

    sides = (
        (a < n_along - 1, (a + 1, c), a > 0),
        (a > 0, (a - 1, c), a < n_along - 1),
        (c < n_across - 1, (a, c + 1), c > 0),
        (c > 0, (a, c - 1), c < n_across - 1),
    )

    def halo(side, device):
        return remote(
            rim, sources.at[blocks + side], halo_send.at[side], halo_recv.at[side], device
        )

    for side, (has_target, device, has_source) in enumerate(sides):

        @pl.when(has_target)
        def _(side=side, device=device):
            halo(side, device).start()

        @pl.when(jnp.logical_not(has_source))
        def _(side=side):
            sources[blocks + side] = jnp.zeros((tile, width), bf16)

    loads[2].wait()
    pool_pick = (
        lax.broadcasted_iota(jnp.int32, (coarse_count, nodes), 0) == pool_row[...]
    ).astype(f32).astype(bf16)
    loads[3].wait()
    cot_all[c] = dot(pool_pick, cotangent[...])
    cot_copies = [
        remote(cot_all.at[c], cot_all.at[c], cot_send.at[d], cot_recv.at[c], (a, peer))
        for d, peer in enumerate(across_peers)
    ]
    for copy in cot_copies:
        copy.start()

    loads[4].wait()
    loads[5].wait()
    w_first = w_update[0:width, :]
    w_second = w_update[width : 2 * width, :]
    w_joined[...] = dot(w_msg[...], w_second).astype(bf16)
    for b in range(blocks):
        pre[b * tile : (b + 1) * tile, :] = dot(sources[b], w_first)

    for load in loads[6:9]:
        load.wait()
    for side, (has_target, device, has_source) in enumerate(sides):

        @pl.when(has_source)
        def _(side=side):
            halo(side, (a, c)).wait_recv()

    pooled = jnp.zeros((coarse_count, width), f32)
    for b in range(blocks):
        rows = slice(b * tile, (b + 1) * tile)
        gathered = jnp.concatenate([sources[adj_index[k, b]] for k in range(slots)], axis=0)
        weights = jnp.concatenate(
            [
                adj[b, k]
                * jnp.where(k < adj_count[0, b], 1.0, 0.0).astype(bf16)
                for k in range(slots)
            ],
            axis=1,
        )
        block_sum = dot(weights, gathered).astype(bf16)
        summed[rows, :] = block_sum
        v = pre[rows, :] + dot(block_sum, w_joined[...])
        s = sigmoid(v)
        slope[rows, :] = s * (1.0 + v * (1.0 - s))
        h = features[rows, :].astype(f32) + v * s
        hidden[rows, :] = h
        high, low = split(h)
        pick = pool_pick[:, rows]
        pooled += dot(pick, high) + dot(pick, low)
    pool_all[c] = pooled
    pool_copies = [
        remote(pool_all.at[c], pool_all.at[c], pool_send.at[d], pool_recv.at[c], (a, peer))
        for d, peer in enumerate(across_peers)
    ]
    for copy in pool_copies:
        copy.start()

    for b in range(blocks):
        rows = slice(b * tile, (b + 1) * tile)
        summed_t[:, rows] = summed[rows, :].T
    loads[9].wait()

    for peer in across_peers:
        remote(
            cot_all.at[peer], cot_all.at[peer], cot_send.at[0], cot_recv.at[peer], (a, c)
        ).wait_recv()
        remote(
            pool_all.at[peer], pool_all.at[peer], pool_send.at[0], pool_recv.at[peer], (a, c)
        ).wait_recv()
    pooled, coarse_cot = pool_all[0], cot_all[0]
    for i in range(1, n_across):
        pooled, coarse_cot = pooled + pool_all[i], coarse_cot + cot_all[i]

    coarse_norm, inverse = normalize(pooled)
    coarse = coarse_norm.astype(bf16)
    coarse_pre = dot(coarse, w_coarse[...])
    s = sigmoid(coarse_pre)
    coarse_out = (coarse_pre * s).astype(bf16)
    coarse_delta = (coarse_cot * (s * (1.0 + coarse_pre * (1.0 - s)))).astype(bf16)
    pack[0:coarse_count, :] = coarse
    pack[coarse_count : 2 * coarse_count, :] = coarse_delta

    def send_pack(target):
        return remote(pack, pack_all.at[a], pack_send.at[target - half], pack_recv.at[a], (target, c))

    for target in range(half, n_along):

        @pl.when(a != target)
        def _(target=target):
            send_pack(target).start()

    coarse_back = times_transposed(coarse_delta, w_coarse[...])
    mean_one = jnp.mean(coarse_back, axis=-1, keepdims=True)
    mean_two = jnp.mean(coarse_back * coarse_norm, axis=-1, keepdims=True)
    pooled_delta = inverse * (coarse_back - mean_one - coarse_norm * mean_two)
    delta_parts = jnp.concatenate(split(pooled_delta), axis=0)
    twice_pick = jnp.concatenate([pool_pick, pool_pick], axis=0)

    for b in range(blocks):
        rows = slice(b * tile, (b + 1) * tile)
        spread = transposed_times(twice_pick[:, rows], delta_parts)
        hidden_delta = cotangent[rows, :].astype(f32) + spread
        update_delta[rows, :] = (hidden_delta * slope[rows, :]).astype(bf16)
    total[...] = dot(summed_t[...], update_delta[...])

    for i in range(half):
        for j in range(n_across):
            start = (i * n_across + j) * chunk
            part[j, i] = total[start : start + chunk, :].astype(bf16)

    def send_part(i, d, peer):
        return remote(
            part.at[peer, i], part_all.at[c, i], part_send.at[d, i], part_recv.at[c, i], (a, peer)
        )

    for i in reversed(range(half)):
        for d, peer in enumerate(across_peers):
            send_part(i, d, peer).start()

    for b in range(blocks):
        rows = slice(b * tile, (b + 1) * tile)
        spread = transposed_times(pool_pick[:, rows], coarse_out)
        updated[rows, :] = (hidden[rows, :] + spread).astype(bf16)
    store = pltpu.make_async_copy(updated, updated_hbm, out_sem.at[0])
    store.start()

    def send_second(i):
        return remote(
            second.at[i], second_all.at[a], second_send.at[i], second_recv.at[a], (i, c)
        )

    for i in reversed(range(half)):
        start = pl.multiple_of((i * n_across + c) * chunk, chunk)
        chunk_sum = total[pl.ds(start, chunk), :]
        for peer in across_peers:
            remote(
                part.at[peer, i], part_all.at[peer, i], part_send.at[0, i], part_recv.at[peer, i], (a, c)
            ).wait_recv()
            chunk_sum = chunk_sum + part_all[peer, i].astype(f32)

        @pl.when(a == i)
        def _(chunk_sum=chunk_sum):
            own_chunk[...] = chunk_sum

        @pl.when(a != i)
        def _(chunk_sum=chunk_sum, i=i):
            second[i] = chunk_sum.astype(bf16)
            send_second(i).start()

    @pl.when(a < half)
    def _():
        chunk_sum = own_chunk[...]
        for peer in along_peers:
            remote(
                second.at[0], second_all.at[peer], second_send.at[0], second_recv.at[peer], (a, c)
            ).wait_recv()
            chunk_sum = chunk_sum + second_all[peer].astype(f32)
        high, low = split(chunk_sum)
        both = times_transposed(jnp.concatenate([high, low], axis=0), w_second)
        put_grads(both[0:chunk, :] + both[chunk : 2 * chunk, :])

    @pl.when(a >= half)
    def _():
        pack_all[a] = pack[...]
        for peer in along_peers:
            remote(
                pack, pack_all.at[peer], pack_send.at[0], pack_recv.at[peer], (a, c)
            ).wait_recv()
        rows = n_along * coarse_count
        all_coarse = pack_all[:, 0:coarse_count, :].reshape(rows, width)
        all_delta = pack_all[:, coarse_count : 2 * coarse_count, :].reshape(rows, width)
        coarse_grad[...] = transposed_times(all_coarse, all_delta)
        start = pl.multiple_of(((a - half) * n_across + c) * chunk, chunk)
        put_grads(coarse_grad[pl.ds(start, chunk), :])

    for side, (has_target, device, has_source) in enumerate(sides):

        @pl.when(has_target)
        def _(side=side, device=device):
            halo(side, device).wait_send()

    for copy in cot_copies + pool_copies:
        copy.wait_send()
    for target in range(half, n_along):

        @pl.when(a != target)
        def _(target=target):
            send_pack(target).wait_send()

    for i in range(half):
        for d, peer in enumerate(across_peers):
            send_part(i, d, peer).wait_send()

        @pl.when(a != i)
        def _(i=i):
            send_second(i).wait_send()

    store.wait()


def fused_layer(
    n_along,
    n_across,
    chunk,
    features,
    adj_tiles,
    adj_index,
    adj_count,
    bnd_index,
    pool_index,
    w_msg,
    w_update,
    w_coarse,
    cotangent,
):
    nodes, width = features.shape
    blocks, slots, tile, _ = adj_tiles.shape
    half = n_along // 2
    coarse_count = NC_DEV * n_across
    vmem = pltpu.VMEM
    dma = pltpu.SemaphoreType.DMA
    hbm_spec = pl.BlockSpec(memory_space=pltpu.HBM)
    vmem_spec = pl.BlockSpec(memory_space=pltpu.VMEM)
    any_spec = pl.BlockSpec(memory_space=pl.ANY)
    updated, grads = pl.pallas_call(
        functools.partial(layer_kernel, n_along, n_across),
        name="mesh_layer",
        out_shape=(
            jax.ShapeDtypeStruct((nodes, width), bf16),
            jax.ShapeDtypeStruct((chunk * width // 128, 128), f32),
        ),
        in_specs=[hbm_spec] * 10,
        out_specs=(any_spec, vmem_spec),
        scratch_shapes=[
            pltpu.SMEM((slots, blocks), jnp.int32),
            pltpu.SMEM((1, blocks), jnp.int32),
            vmem((1, tile), jnp.int32),
            vmem((1, nodes), jnp.int32),
            vmem((nodes, width), bf16),
            vmem(adj_tiles.shape, bf16),
            vmem(w_msg.shape, bf16),
            vmem(w_update.shape, bf16),
            vmem(w_coarse.shape, bf16),
            vmem((nodes, width), bf16),
            vmem((blocks + 4, tile, width), bf16),
            vmem((tile, width), bf16),
            vmem((width, width), bf16),
            vmem((nodes, width), f32),
            vmem((nodes, width), f32),
            vmem((nodes, width), f32),
            vmem((nodes, width), bf16),
            vmem((width, nodes), bf16),
            vmem((nodes, width), bf16),
            vmem((nodes, width), bf16),
            vmem((n_across, coarse_count, width), f32),
            vmem((n_across, coarse_count, width), f32),
            vmem((2 * coarse_count, width), bf16),
            vmem((n_along, 2 * coarse_count, width), bf16),
            vmem((width, width), f32),
            vmem((width, width), f32),
            vmem((n_across, half, chunk, width), bf16),
            vmem((n_across, half, chunk, width), bf16),
            vmem((half, chunk, width), bf16),
            vmem((n_along, chunk, width), bf16),
            vmem((chunk, width), f32),
            dma((10,)),
            dma((1,)),
            dma((4,)),
            dma((4,)),
            dma((n_across,)),
            dma((n_across,)),
            dma((n_across,)),
            dma((n_across,)),
            dma((half,)),
            dma((n_along,)),
            dma((n_across, half)),
            dma((n_across, half)),
            dma((half,)),
            dma((n_along,)),
        ],
        compiler_params=pltpu.CompilerParams(
            collective_id=0, has_side_effects=True, vmem_limit_bytes=60 * 2**20
        ),
        cost_estimate=pl.CostEstimate(
            flops=2 * nodes * width * (slots * tile + 5 * width),
            bytes_accessed=4 * 2**20,
            transcendentals=nodes * width,
        ),
    )(
        adj_index.T,
        adj_count.reshape(1, blocks),
        bnd_index.reshape(1, tile),
        pool_index.reshape(1, nodes),
        features,
        adj_tiles,
        w_msg,
        w_update,
        w_coarse,
        cotangent,
    )
    return updated, grads.reshape(-1)


def layer(axes, features, adj_tiles, *others):
    n_along, n_across = axes["along"], axes["across"]
    width = features.shape[1]
    chunk = 2 * width // (n_along * n_across)
    if n_along % 2 == 0 and chunk and chunk % 16 == 0:
        return fused_layer(n_along, n_across, chunk, features, adj_tiles, *others)
    return plain_layer(features, adj_tiles, *others)


def solution(mesh):
    return jax.shard_map(
        functools.partial(layer, dict(mesh.shape)),
        mesh=mesh,
        in_specs=(
            P(("along", "across"), None),
            P(("along", "across"), None, None, None),
            P(("along", "across"), None),
            P(("along", "across")),
            P(("along", "across")),
            P(("along", "across")),
            P(),
            P(),
            P(),
            P(("along", "across"), None),
        ),
        out_specs=(P(("along", "across"), None), P(("along", "across"))),
        check_vma=False,
    )
```

```python
import functools

import jax
import jax.numpy as jnp
from jax import lax
from jax.experimental import pallas as pl
from jax.experimental.pallas import tpu as pltpu
from jax.sharding import PartitionSpec as P

NC_DEV = 4


eps = 1e-05


def extended(block, sides, width):
    for axis, dim in sides:
        count = lax.axis_size(axis)
        forward = [(i, i + 1) for i in range(count - 1)]
        backward = [(target, source) for source, target in forward]
        low = lax.ppermute(
            lax.slice_in_dim(block, block.shape[dim] - width, None, axis=dim), axis, forward
        )
        high = lax.ppermute(lax.slice_in_dim(block, 0, width, axis=dim), axis, backward)
        block = jnp.concatenate([low, block, high], axis=dim)
    return block


def normalize(values):
    center = values - jnp.mean(values, axis=-1, keepdims=True)
    inverse = lax.rsqrt(jnp.mean(center * center, axis=-1, keepdims=True) + eps)
    return (center * inverse, inverse)


def silu_slope(values):
    logistic = jax.nn.sigmoid(values)
    return logistic * (1.0 + values * (1.0 - logistic))


def transposed_times(operand, second, precision=None):
    return lax.dot_general(
        operand,
        second,
        (((0,), (0,)), ((), ())),
        precision=precision,
        preferred_element_type=jnp.float32,
    )


def times_transposed(operand, second):
    return lax.dot_general(
        operand, second, (((1,), (1,)), ((), ())), preferred_element_type=jnp.float32
    )


def coarse_forward(pooled, w_coarse):
    coarse_norm, inverse = normalize(pooled)
    coarse = coarse_norm.astype(jnp.bfloat16)
    coarse_pre = jnp.dot(coarse, w_coarse, preferred_element_type=jnp.float32)
    return (coarse_norm, inverse, coarse, coarse_pre, jax.nn.silu(coarse_pre).astype(jnp.bfloat16))


def coarse_backward(coarse_cot, coarse_norm, inverse, coarse_pre, w_coarse):
    coarse_delta = (coarse_cot * silu_slope(coarse_pre)).astype(jnp.bfloat16)
    coarse_back = times_transposed(coarse_delta, w_coarse)
    mean_one = jnp.mean(coarse_back, axis=-1, keepdims=True)
    mean_two = jnp.mean(coarse_back * coarse_norm, axis=-1, keepdims=True)
    return (coarse_delta, inverse * (coarse_back - mean_one - coarse_norm * mean_two))


def plain_layer(
    features,
    adj_tiles,
    adj_index,
    adj_count,
    bnd_index,
    pool_index,
    w_msg,
    w_update,
    w_coarse,
    cotangent,
):
    feature_count = features.shape[1]
    blocks = adj_tiles.shape[0]
    slot_count = adj_tiles.shape[1]
    tile_rows = adj_tiles.shape[2]
    inputs = features.astype(jnp.float32)
    normed, _ = normalize(inputs)
    scaled = normed.astype(jnp.bfloat16)
    rim_rows = scaled[bnd_index]
    padded = extended(rim_rows[None, None], (("along", 0), ("across", 1)), 1)
    halo_tiles = jnp.stack([padded[0, 1], padded[2, 1], padded[1, 0], padded[1, 2]])
    sources = jnp.concatenate(
        [scaled.reshape(blocks, tile_rows, feature_count), halo_tiles], axis=0
    )
    messages = jnp.dot(
        sources.reshape(-1, feature_count), w_msg, preferred_element_type=jnp.float32
    )
    messages = messages.astype(jnp.bfloat16).reshape(sources.shape)
    live_slots = jnp.arange(slot_count)[None, :] < adj_count[:, None]
    masked_tiles = jnp.where(live_slots[:, :, None, None], adj_tiles, jnp.zeros((), jnp.bfloat16))
    aggregated = jnp.einsum(
        "bkij,bkjh->bih", masked_tiles, messages[adj_index], preferred_element_type=jnp.float32
    )
    aggregated = aggregated.astype(jnp.bfloat16).reshape(-1, feature_count)
    summed_scaled = jnp.einsum(
        "bkij,bkjh->bih", masked_tiles, sources[adj_index], preferred_element_type=jnp.float32
    )
    summed_scaled = summed_scaled.astype(jnp.bfloat16).reshape(-1, feature_count)
    w_first = w_update[:feature_count]
    w_second = w_update[feature_count:]
    update_pre = jnp.dot(scaled, w_first, preferred_element_type=jnp.float32) + jnp.dot(
        aggregated, w_second, preferred_element_type=jnp.float32
    )
    hidden_one = inputs + jax.nn.silu(update_pre)
    coarse_count = NC_DEV * lax.axis_size("across")
    assign_float = (pool_index[:, None] == jnp.arange(coarse_count)[None, :]).astype(jnp.float32)
    assign_bits = assign_float.astype(jnp.bfloat16)
    pooled_part = transposed_times(assign_float, hidden_one, lax.Precision.HIGHEST)
    cot_part = transposed_times(assign_bits, cotangent)
    pooled, coarse_cot = lax.psum((pooled_part, cot_part), "across")
    coarse_norm, inverse, coarse, coarse_pre, coarse_out = coarse_forward(pooled, w_coarse)
    hidden_two = hidden_one + jnp.dot(assign_bits, coarse_out, preferred_element_type=jnp.float32)
    coarse_delta, pooled_delta = coarse_backward(
        coarse_cot, coarse_norm, inverse, coarse_pre, w_coarse
    )
    start = lax.axis_index("across") * NC_DEV
    own_coarse = lax.dynamic_slice_in_dim(coarse, start, NC_DEV, 0)
    own_coarse_delta = lax.dynamic_slice_in_dim(coarse_delta, start, NC_DEV, 0)
    coarse_grad = transposed_times(own_coarse, own_coarse_delta)
    hidden_delta = cotangent.astype(jnp.float32) + jnp.dot(
        assign_float,
        pooled_delta,
        precision=lax.Precision.HIGHEST,
        preferred_element_type=jnp.float32,
    )
    update_delta = (hidden_delta * silu_slope(update_pre)).astype(jnp.bfloat16)
    aggregated_delta = times_transposed(update_delta, w_second).astype(jnp.bfloat16)
    message_grad = transposed_times(summed_scaled, aggregated_delta)
    grad_terms = jnp.concatenate([message_grad.reshape(-1), coarse_grad.reshape(-1)])
    partial_grads = lax.psum_scatter(grad_terms, "along", scatter_dimension=0, tiled=True)
    weight_grads = lax.psum_scatter(partial_grads, "across", scatter_dimension=0, tiled=True)
    return (hidden_two.astype(jnp.bfloat16), weight_grads)


MESH = pl.DeviceIdType.MESH
f32 = jnp.float32
bf16 = jnp.bfloat16


def split(values):
    high = values.astype(bf16)
    return high, (values - high.astype(f32)).astype(bf16)


def dot(first, second):
    return jnp.dot(first, second, preferred_element_type=f32)


def sigmoid(values):
    return 0.5 * jnp.tanh(0.5 * values) + 0.5


def layer_kernel(
    n_along,
    n_across,
    index_hbm,
    count_hbm,
    bnd_hbm,
    pool_hbm,
    features_hbm,
    adj_hbm,
    w_msg_hbm,
    w_update_hbm,
    w_coarse_hbm,
    cotangent_hbm,
    updated_hbm,
    grads,
    adj_index,
    adj_count,
    bnd_row,
    pool_row,
    features,
    adj,
    w_msg,
    w_update,
    w_coarse,
    cotangent,
    sources,
    rim,
    w_joined,
    pre,
    hidden,
    slope,
    summed,
    summed_t,
    update_delta,
    updated,
    pool_all,
    cot_all,
    pack,
    pack_all,
    coarse_grad,
    total,
    part,
    part_all,
    second,
    second_all,
    own_chunk,
    in_sem,
    out_sem,
    halo_send,
    halo_recv,
    pool_send,
    pool_recv,
    cot_send,
    cot_recv,
    pack_send,
    pack_recv,
    part_send,
    part_recv,
    second_send,
    second_recv,
):
    a = lax.axis_index("along")
    c = lax.axis_index("across")
    half = n_along // 2
    nodes, width = features.shape
    blocks, slots, tile, _ = adj.shape
    coarse_count = NC_DEV * n_across
    chunk = own_chunk.shape[0]

    def put_grads(values):
        lanes = grads.shape[1]
        parts = width // lanes
        for i in range(parts):
            grads[pl.ds(i, chunk, stride=parts), :] = values[:, i * lanes : (i + 1) * lanes]

    loads = [
        pltpu.make_async_copy(source, target, in_sem.at[i])
        for i, (source, target) in enumerate(
            (
                (features_hbm, features),
                (bnd_hbm, bnd_row),
                (pool_hbm, pool_row),
                (cotangent_hbm, cotangent),
                (w_update_hbm, w_update),
                (w_msg_hbm, w_msg),
                (index_hbm, adj_index),
                (count_hbm, adj_count),
                (adj_hbm, adj),
                (w_coarse_hbm, w_coarse),
            )
        )
    ]
    for load in loads:
        load.start()

    barrier = pltpu.get_barrier_semaphore()
    across_peers = [lax.rem(c + d, n_across) for d in range(1, n_across)]
    along_peers = [lax.rem(a + d, n_along) for d in range(1, n_along)]
    for peer in across_peers:
        pl.semaphore_signal(barrier, inc=1, device_id=(a, peer), device_id_type=MESH)
    for peer in along_peers:
        pl.semaphore_signal(barrier, inc=1, device_id=(peer, c), device_id_type=MESH)

    def remote(source, target, send, recv, device):
        return pltpu.make_async_remote_copy(
            src_ref=source,
            dst_ref=target,
            send_sem=send,
            recv_sem=recv,
            device_id=device,
            device_id_type=MESH,
        )

    loads[1].wait()
    bnd_column = jnp.broadcast_to(bnd_row[...].astype(f32), (tile, tile)).T[:, 0:1]
    lanes = lax.broadcasted_iota(jnp.int32, (tile, nodes), 1)
    rim_pick = (lanes == bnd_column.astype(jnp.int32)).astype(f32).astype(bf16)
    loads[0].wait()
    rim[...] = normalize(dot(rim_pick, features[...]))[0].astype(bf16)

    pl.semaphore_wait(barrier, n_across - 1 + n_along - 1)

    sides = (
        (a < n_along - 1, (a + 1, c), a > 0),
        (a > 0, (a - 1, c), a < n_along - 1),
        (c < n_across - 1, (a, c + 1), c > 0),
        (c > 0, (a, c - 1), c < n_across - 1),
    )

    def halo(side, device):
        return remote(
            rim, sources.at[blocks + side], halo_send.at[side], halo_recv.at[side], device
        )

    for side, (has_target, device, has_source) in enumerate(sides):

        @pl.when(has_target)
        def _(side=side, device=device):
            halo(side, device).start()

        @pl.when(jnp.logical_not(has_source))
        def _(side=side):
            sources[blocks + side] = jnp.zeros((tile, width), bf16)

    for b in range(blocks):
        x = features[b * tile : (b + 1) * tile, :].astype(f32)
        sources[b] = normalize(x)[0].astype(bf16)

    loads[2].wait()
    pool_pick = (
        lax.broadcasted_iota(jnp.int32, (coarse_count, nodes), 0) == pool_row[...]
    ).astype(f32).astype(bf16)
    loads[3].wait()
    cot_all[c] = dot(pool_pick, cotangent[...])
    cot_copies = [
        remote(cot_all.at[c], cot_all.at[c], cot_send.at[d], cot_recv.at[c], (a, peer))
        for d, peer in enumerate(across_peers)
    ]
    for copy in cot_copies:
        copy.start()

    loads[4].wait()
    loads[5].wait()
    w_first = w_update[0:width, :]
    w_second = w_update[width : 2 * width, :]
    w_joined[...] = dot(w_msg[...], w_second).astype(bf16)
    pre[...] = dot(sources[0:blocks].reshape(nodes, width), w_first)

    for load in loads[6:9]:
        load.wait()
    for side, (has_target, device, has_source) in enumerate(sides):

        @pl.when(has_source)
        def _(side=side):
            halo(side, (a, c)).wait_recv()

    pooled = jnp.zeros((coarse_count, width), f32)
    for b in range(blocks):
        rows = slice(b * tile, (b + 1) * tile)
        gathered = jnp.concatenate([sources[adj_index[k, b]] for k in range(slots)], axis=0)
        weights = jnp.concatenate(
            [
                adj[b, k]
                * jnp.where(k < adj_count[0, b], 1.0, 0.0).astype(bf16)
                for k in range(slots)
            ],
            axis=1,
        )
        block_sum = dot(weights, gathered).astype(bf16)
        summed[rows, :] = block_sum
        v = pre[rows, :] + dot(block_sum, w_joined[...])
        s = sigmoid(v)
        slope[rows, :] = s * (1.0 + v * (1.0 - s))
        h = features[rows, :].astype(f32) + v * s
        hidden[rows, :] = h
        high, low = split(h)
        pick = pool_pick[:, rows]
        pooled += dot(pick, high) + dot(pick, low)
    pool_all[c] = pooled
    pool_copies = [
        remote(pool_all.at[c], pool_all.at[c], pool_send.at[d], pool_recv.at[c], (a, peer))
        for d, peer in enumerate(across_peers)
    ]
    for copy in pool_copies:
        copy.start()

    for b in range(blocks):
        rows = slice(b * tile, (b + 1) * tile)
        summed_t[:, rows] = summed[rows, :].T
    loads[9].wait()

    for peer in across_peers:
        remote(
            cot_all.at[peer], cot_all.at[peer], cot_send.at[0], cot_recv.at[peer], (a, c)
        ).wait_recv()
        remote(
            pool_all.at[peer], pool_all.at[peer], pool_send.at[0], pool_recv.at[peer], (a, c)
        ).wait_recv()
    pooled, coarse_cot = pool_all[0], cot_all[0]
    for i in range(1, n_across):
        pooled, coarse_cot = pooled + pool_all[i], coarse_cot + cot_all[i]

    coarse_norm, inverse = normalize(pooled)
    coarse = coarse_norm.astype(bf16)
    coarse_pre = dot(coarse, w_coarse[...])
    s = sigmoid(coarse_pre)
    coarse_out = (coarse_pre * s).astype(bf16)
    coarse_delta = (coarse_cot * (s * (1.0 + coarse_pre * (1.0 - s)))).astype(bf16)
    pack[0:coarse_count, :] = coarse
    pack[coarse_count : 2 * coarse_count, :] = coarse_delta

    def send_pack(target):
        return remote(pack, pack_all.at[a], pack_send.at[target - half], pack_recv.at[a], (target, c))

    for target in range(half, n_along):

        @pl.when(a != target)
        def _(target=target):
            send_pack(target).start()

    coarse_back = times_transposed(coarse_delta, w_coarse[...])
    mean_one = jnp.mean(coarse_back, axis=-1, keepdims=True)
    mean_two = jnp.mean(coarse_back * coarse_norm, axis=-1, keepdims=True)
    pooled_delta = inverse * (coarse_back - mean_one - coarse_norm * mean_two)
    delta_parts = jnp.concatenate(split(pooled_delta), axis=0)
    twice_pick = jnp.concatenate([pool_pick, pool_pick], axis=0)

    for b in range(blocks):
        rows = slice(b * tile, (b + 1) * tile)
        spread = transposed_times(twice_pick[:, rows], delta_parts)
        hidden_delta = cotangent[rows, :].astype(f32) + spread
        update_delta[rows, :] = (hidden_delta * slope[rows, :]).astype(bf16)
    total[...] = dot(summed_t[...], update_delta[...])

    for i in range(half):
        for j in range(n_across):
            start = (i * n_across + j) * chunk
            part[j, i] = total[start : start + chunk, :].astype(bf16)

    def send_part(i, d, peer):
        return remote(
            part.at[peer, i], part_all.at[c, i], part_send.at[d, i], part_recv.at[c, i], (a, peer)
        )

    for i in reversed(range(half)):
        for d, peer in enumerate(across_peers):
            send_part(i, d, peer).start()

    for b in range(blocks):
        rows = slice(b * tile, (b + 1) * tile)
        spread = transposed_times(pool_pick[:, rows], coarse_out)
        updated[rows, :] = (hidden[rows, :] + spread).astype(bf16)
    store = pltpu.make_async_copy(updated, updated_hbm, out_sem.at[0])
    store.start()

    def send_second(i):
        return remote(
            second.at[i], second_all.at[a], second_send.at[i], second_recv.at[a], (i, c)
        )

    for i in reversed(range(half)):
        start = pl.multiple_of((i * n_across + c) * chunk, chunk)
        chunk_sum = total[pl.ds(start, chunk), :]
        for peer in across_peers:
            remote(
                part.at[peer, i], part_all.at[peer, i], part_send.at[0, i], part_recv.at[peer, i], (a, c)
            ).wait_recv()
            chunk_sum = chunk_sum + part_all[peer, i].astype(f32)

        @pl.when(a == i)
        def _(chunk_sum=chunk_sum):
            own_chunk[...] = chunk_sum

        @pl.when(a != i)
        def _(chunk_sum=chunk_sum, i=i):
            second[i] = chunk_sum.astype(bf16)
            send_second(i).start()

    @pl.when(a < half)
    def _():
        chunk_sum = own_chunk[...]
        for peer in along_peers:
            remote(
                second.at[0], second_all.at[peer], second_send.at[0], second_recv.at[peer], (a, c)
            ).wait_recv()
            chunk_sum = chunk_sum + second_all[peer].astype(f32)
        high, low = split(chunk_sum)
        both = times_transposed(jnp.concatenate([high, low], axis=0), w_second)
        put_grads(both[0:chunk, :] + both[chunk : 2 * chunk, :])

    @pl.when(a >= half)
    def _():
        pack_all[a] = pack[...]
        for peer in along_peers:
            remote(
                pack, pack_all.at[peer], pack_send.at[0], pack_recv.at[peer], (a, c)
            ).wait_recv()
        rows = n_along * coarse_count
        all_coarse = pack_all[:, 0:coarse_count, :].reshape(rows, width)
        all_delta = pack_all[:, coarse_count : 2 * coarse_count, :].reshape(rows, width)
        coarse_grad[...] = transposed_times(all_coarse, all_delta)
        start = pl.multiple_of(((a - half) * n_across + c) * chunk, chunk)
        put_grads(coarse_grad[pl.ds(start, chunk), :])

    for side, (has_target, device, has_source) in enumerate(sides):

        @pl.when(has_target)
        def _(side=side, device=device):
            halo(side, device).wait_send()

    for copy in cot_copies + pool_copies:
        copy.wait_send()
    for target in range(half, n_along):

        @pl.when(a != target)
        def _(target=target):
            send_pack(target).wait_send()

    for i in range(half):
        for d, peer in enumerate(across_peers):
            send_part(i, d, peer).wait_send()

        @pl.when(a != i)
        def _(i=i):
            send_second(i).wait_send()

    store.wait()


def fused_layer(
    n_along,
    n_across,
    chunk,
    features,
    adj_tiles,
    adj_index,
    adj_count,
    bnd_index,
    pool_index,
    w_msg,
    w_update,
    w_coarse,
    cotangent,
):
    nodes, width = features.shape
    blocks, slots, tile, _ = adj_tiles.shape
    half = n_along // 2
    coarse_count = NC_DEV * n_across
    vmem = pltpu.VMEM
    dma = pltpu.SemaphoreType.DMA
    hbm_spec = pl.BlockSpec(memory_space=pltpu.HBM)
    vmem_spec = pl.BlockSpec(memory_space=pltpu.VMEM)
    any_spec = pl.BlockSpec(memory_space=pl.ANY)
    updated, grads = pl.pallas_call(
        functools.partial(layer_kernel, n_along, n_across),
        name="mesh_layer",
        out_shape=(
            vmem((nodes, width), bf16),
            vmem((chunk * width // 128, 128), f32),
        ),
        in_specs=[hbm_spec] * 10,
        out_specs=(any_spec, vmem_spec),
        scratch_shapes=[
            pltpu.SMEM((slots, blocks), jnp.int32),
            pltpu.SMEM((1, blocks), jnp.int32),
            vmem((1, tile), jnp.int32),
            vmem((1, nodes), jnp.int32),
            vmem((nodes, width), bf16),
            vmem(adj_tiles.shape, bf16),
            vmem(w_msg.shape, bf16),
            vmem(w_update.shape, bf16),
            vmem(w_coarse.shape, bf16),
            vmem((nodes, width), bf16),
            vmem((blocks + 4, tile, width), bf16),
            vmem((tile, width), bf16),
            vmem((width, width), bf16),
            vmem((nodes, width), f32),
            vmem((nodes, width), f32),
            vmem((nodes, width), f32),
            vmem((nodes, width), bf16),
            vmem((width, nodes), bf16),
            vmem((nodes, width), bf16),
            vmem((nodes, width), bf16),
            vmem((n_across, coarse_count, width), f32),
            vmem((n_across, coarse_count, width), f32),
            vmem((2 * coarse_count, width), bf16),
            vmem((n_along, 2 * coarse_count, width), bf16),
            vmem((width, width), f32),
            vmem((width, width), f32),
            vmem((n_across, half, chunk, width), bf16),
            vmem((n_across, half, chunk, width), bf16),
            vmem((half, chunk, width), bf16),
            vmem((n_along, chunk, width), bf16),
            vmem((chunk, width), f32),
            dma((10,)),
            dma((1,)),
            dma((4,)),
            dma((4,)),
            dma((n_across,)),
            dma((n_across,)),
            dma((n_across,)),
            dma((n_across,)),
            dma((half,)),
            dma((n_along,)),
            dma((n_across, half)),
            dma((n_across, half)),
            dma((half,)),
            dma((n_along,)),
        ],
        compiler_params=pltpu.CompilerParams(
            collective_id=0, has_side_effects=True, vmem_limit_bytes=60 * 2**20
        ),
        cost_estimate=pl.CostEstimate(
            flops=2 * nodes * width * (slots * tile + 5 * width),
            bytes_accessed=4 * 2**20,
            transcendentals=nodes * width,
        ),
    )(
        adj_index.T,
        adj_count.reshape(1, blocks),
        bnd_index.reshape(1, tile),
        pool_index.reshape(1, nodes),
        features,
        adj_tiles,
        w_msg,
        w_update,
        w_coarse,
        cotangent,
    )
    return updated, grads.reshape(-1)


def layer(axes, features, adj_tiles, *others):
    n_along, n_across = axes["along"], axes["across"]
    width = features.shape[1]
    chunk = 2 * width // (n_along * n_across)
    if n_along % 2 == 0 and chunk and chunk % 16 == 0:
        return fused_layer(n_along, n_across, chunk, features, adj_tiles, *others)
    return plain_layer(features, adj_tiles, *others)


def solution(mesh):
    return jax.shard_map(
        functools.partial(layer, dict(mesh.shape)),
        mesh=mesh,
        in_specs=(
            P(("along", "across"), None),
            P(("along", "across"), None, None, None),
            P(("along", "across"), None),
            P(("along", "across")),
            P(("along", "across")),
            P(("along", "across")),
            P(),
            P(),
            P(),
            P(("along", "across"), None),
        ),
        out_specs=(P(("along", "across"), None), P(("along", "across"))),
        check_vma=False,
    )
```

```python
import functools

import jax
import jax.numpy as jnp
from jax import lax
from jax.experimental import pallas as pl
from jax.experimental.pallas import tpu as pltpu
from jax.sharding import PartitionSpec as P

NC_DEV = 4


eps = 1e-05


def extended(block, sides, width):
    for axis, dim in sides:
        count = lax.axis_size(axis)
        forward = [(i, i + 1) for i in range(count - 1)]
        backward = [(target, source) for source, target in forward]
        low = lax.ppermute(
            lax.slice_in_dim(block, block.shape[dim] - width, None, axis=dim), axis, forward
        )
        high = lax.ppermute(lax.slice_in_dim(block, 0, width, axis=dim), axis, backward)
        block = jnp.concatenate([low, block, high], axis=dim)
    return block


def normalize(values):
    center = values - jnp.mean(values, axis=-1, keepdims=True)
    inverse = lax.rsqrt(jnp.mean(center * center, axis=-1, keepdims=True) + eps)
    return (center * inverse, inverse)


def silu_slope(values):
    logistic = jax.nn.sigmoid(values)
    return logistic * (1.0 + values * (1.0 - logistic))


def transposed_times(operand, second, precision=None):
    return lax.dot_general(
        operand,
        second,
        (((0,), (0,)), ((), ())),
        precision=precision,
        preferred_element_type=jnp.float32,
    )


def times_transposed(operand, second):
    return lax.dot_general(
        operand, second, (((1,), (1,)), ((), ())), preferred_element_type=jnp.float32
    )


def coarse_forward(pooled, w_coarse):
    coarse_norm, inverse = normalize(pooled)
    coarse = coarse_norm.astype(jnp.bfloat16)
    coarse_pre = jnp.dot(coarse, w_coarse, preferred_element_type=jnp.float32)
    return (coarse_norm, inverse, coarse, coarse_pre, jax.nn.silu(coarse_pre).astype(jnp.bfloat16))


def coarse_backward(coarse_cot, coarse_norm, inverse, coarse_pre, w_coarse):
    coarse_delta = (coarse_cot * silu_slope(coarse_pre)).astype(jnp.bfloat16)
    coarse_back = times_transposed(coarse_delta, w_coarse)
    mean_one = jnp.mean(coarse_back, axis=-1, keepdims=True)
    mean_two = jnp.mean(coarse_back * coarse_norm, axis=-1, keepdims=True)
    return (coarse_delta, inverse * (coarse_back - mean_one - coarse_norm * mean_two))


def plain_layer(
    features,
    adj_tiles,
    adj_index,
    adj_count,
    bnd_index,
    pool_index,
    w_msg,
    w_update,
    w_coarse,
    cotangent,
):
    feature_count = features.shape[1]
    blocks = adj_tiles.shape[0]
    slot_count = adj_tiles.shape[1]
    tile_rows = adj_tiles.shape[2]
    inputs = features.astype(jnp.float32)
    normed, _ = normalize(inputs)
    scaled = normed.astype(jnp.bfloat16)
    rim_rows = scaled[bnd_index]
    padded = extended(rim_rows[None, None], (("along", 0), ("across", 1)), 1)
    halo_tiles = jnp.stack([padded[0, 1], padded[2, 1], padded[1, 0], padded[1, 2]])
    sources = jnp.concatenate(
        [scaled.reshape(blocks, tile_rows, feature_count), halo_tiles], axis=0
    )
    messages = jnp.dot(
        sources.reshape(-1, feature_count), w_msg, preferred_element_type=jnp.float32
    )
    messages = messages.astype(jnp.bfloat16).reshape(sources.shape)
    live_slots = jnp.arange(slot_count)[None, :] < adj_count[:, None]
    masked_tiles = jnp.where(live_slots[:, :, None, None], adj_tiles, jnp.zeros((), jnp.bfloat16))
    aggregated = jnp.einsum(
        "bkij,bkjh->bih", masked_tiles, messages[adj_index], preferred_element_type=jnp.float32
    )
    aggregated = aggregated.astype(jnp.bfloat16).reshape(-1, feature_count)
    summed_scaled = jnp.einsum(
        "bkij,bkjh->bih", masked_tiles, sources[adj_index], preferred_element_type=jnp.float32
    )
    summed_scaled = summed_scaled.astype(jnp.bfloat16).reshape(-1, feature_count)
    w_first = w_update[:feature_count]
    w_second = w_update[feature_count:]
    update_pre = jnp.dot(scaled, w_first, preferred_element_type=jnp.float32) + jnp.dot(
        aggregated, w_second, preferred_element_type=jnp.float32
    )
    hidden_one = inputs + jax.nn.silu(update_pre)
    coarse_count = NC_DEV * lax.axis_size("across")
    assign_float = (pool_index[:, None] == jnp.arange(coarse_count)[None, :]).astype(jnp.float32)
    assign_bits = assign_float.astype(jnp.bfloat16)
    pooled_part = transposed_times(assign_float, hidden_one, lax.Precision.HIGHEST)
    cot_part = transposed_times(assign_bits, cotangent)
    pooled, coarse_cot = lax.psum((pooled_part, cot_part), "across")
    coarse_norm, inverse, coarse, coarse_pre, coarse_out = coarse_forward(pooled, w_coarse)
    hidden_two = hidden_one + jnp.dot(assign_bits, coarse_out, preferred_element_type=jnp.float32)
    coarse_delta, pooled_delta = coarse_backward(
        coarse_cot, coarse_norm, inverse, coarse_pre, w_coarse
    )
    start = lax.axis_index("across") * NC_DEV
    own_coarse = lax.dynamic_slice_in_dim(coarse, start, NC_DEV, 0)
    own_coarse_delta = lax.dynamic_slice_in_dim(coarse_delta, start, NC_DEV, 0)
    coarse_grad = transposed_times(own_coarse, own_coarse_delta)
    hidden_delta = cotangent.astype(jnp.float32) + jnp.dot(
        assign_float,
        pooled_delta,
        precision=lax.Precision.HIGHEST,
        preferred_element_type=jnp.float32,
    )
    update_delta = (hidden_delta * silu_slope(update_pre)).astype(jnp.bfloat16)
    aggregated_delta = times_transposed(update_delta, w_second).astype(jnp.bfloat16)
    message_grad = transposed_times(summed_scaled, aggregated_delta)
    grad_terms = jnp.concatenate([message_grad.reshape(-1), coarse_grad.reshape(-1)])
    partial_grads = lax.psum_scatter(grad_terms, "along", scatter_dimension=0, tiled=True)
    weight_grads = lax.psum_scatter(partial_grads, "across", scatter_dimension=0, tiled=True)
    return (hidden_two.astype(jnp.bfloat16), weight_grads)


MESH = pl.DeviceIdType.MESH
f32 = jnp.float32
bf16 = jnp.bfloat16


def split(values):
    high = values.astype(bf16)
    return high, (values - high.astype(f32)).astype(bf16)


def dot(first, second):
    return jnp.dot(first, second, preferred_element_type=f32)


def sigmoid(values):
    return 0.5 * jnp.tanh(0.5 * values) + 0.5


def layer_kernel(
    n_along,
    n_across,
    index_hbm,
    count_hbm,
    bnd_hbm,
    pool_hbm,
    features_hbm,
    adj_hbm,
    w_msg_hbm,
    w_update_hbm,
    w_coarse_hbm,
    cotangent_hbm,
    updated_hbm,
    grads,
    adj_index,
    adj_count,
    bnd_row,
    pool_row,
    features,
    adj,
    w_msg,
    w_update,
    w_coarse,
    cotangent,
    sources,
    rim,
    w_joined,
    pre,
    hidden,
    slope,
    summed,
    summed_t,
    picks,
    updated,
    pool_all,
    cot_all,
    pack,
    pack_all,
    coarse_grad,
    total,
    part,
    part_all,
    second,
    second_all,
    own_chunk,
    in_sem,
    out_sem,
    halo_send,
    halo_recv,
    pool_send,
    pool_recv,
    cot_send,
    cot_recv,
    pack_send,
    pack_recv,
    part_send,
    part_recv,
    second_send,
    second_recv,
):
    a = lax.axis_index("along")
    c = lax.axis_index("across")
    half = n_along // 2
    nodes, width = features.shape
    blocks, slots, tile, _ = adj.shape
    coarse_count = NC_DEV * n_across
    chunk = own_chunk.shape[0]

    def put_grads(values):
        lanes = grads.shape[1]
        parts = width // lanes
        for i in range(parts):
            grads[pl.ds(i, chunk, stride=parts), :] = values[:, i * lanes : (i + 1) * lanes]

    loads = [
        pltpu.make_async_copy(source, target, in_sem.at[i])
        for i, (source, target) in enumerate(
            (
                (features_hbm, features),
                (bnd_hbm, bnd_row),
                (pool_hbm, pool_row),
                (cotangent_hbm, cotangent),
                (w_update_hbm, w_update),
                (w_msg_hbm, w_msg),
                (index_hbm, adj_index),
                (count_hbm, adj_count),
                (adj_hbm, adj),
                (w_coarse_hbm, w_coarse),
            )
        )
    ]
    for load in loads:
        load.start()

    barrier = pltpu.get_barrier_semaphore()
    across_peers = [lax.rem(c + d, n_across) for d in range(1, n_across)]
    along_peers = [lax.rem(a + d, n_along) for d in range(1, n_along)]
    for peer in across_peers:
        pl.semaphore_signal(barrier, inc=1, device_id=(a, peer), device_id_type=MESH)
    for peer in along_peers:
        pl.semaphore_signal(barrier, inc=1, device_id=(peer, c), device_id_type=MESH)

    def remote(source, target, send, recv, device):
        return pltpu.make_async_remote_copy(
            src_ref=source,
            dst_ref=target,
            send_sem=send,
            recv_sem=recv,
            device_id=device,
            device_id_type=MESH,
        )

    loads[1].wait()
    bnd_column = jnp.broadcast_to(bnd_row[...].astype(f32), (tile, tile)).T[:, 0:1]
    lanes = lax.broadcasted_iota(jnp.int32, (tile, nodes), 1)
    rim_pick = (lanes == bnd_column.astype(jnp.int32)).astype(f32).astype(bf16)
    loads[0].wait()
    rim[...] = normalize(dot(rim_pick, features[...]))[0].astype(bf16)

    pl.semaphore_wait(barrier, n_across - 1 + n_along - 1)

    sides = (
        (a < n_along - 1, (a + 1, c), a > 0),
        (a > 0, (a - 1, c), a < n_along - 1),
        (c < n_across - 1, (a, c + 1), c > 0),
        (c > 0, (a, c - 1), c < n_across - 1),
    )

    def halo(side, device):
        return remote(
            rim, sources.at[blocks + side], halo_send.at[side], halo_recv.at[side], device
        )

    for side, (has_target, device, has_source) in enumerate(sides):

        @pl.when(has_target)
        def _(side=side, device=device):
            halo(side, device).start()

        @pl.when(jnp.logical_not(has_source))
        def _(side=side):
            sources[blocks + side] = jnp.zeros((tile, width), bf16)

    for load in loads[2:6]:
        load.wait()
    pool_pick = (
        lax.broadcasted_iota(jnp.int32, (coarse_count, nodes), 0) == pool_row[...]
    ).astype(f32).astype(bf16)
    picks[0:coarse_count, :] = pool_pick
    picks[coarse_count : 2 * coarse_count, :] = pool_pick
    w_first = w_update[0:width, :]
    w_second = w_update[width : 2 * width, :]

    def tile_rows(b, count=1):
        size = count * tile
        return pl.ds(pl.multiple_of(b * size, size), size)

    def prepare(b, cot_part):
        rows = tile_rows(b)
        scaled = normalize(features[rows, :].astype(f32))[0].astype(bf16)
        sources[b] = scaled
        pre[rows, :] = dot(scaled, w_first)
        return cot_part + dot(picks[0:coarse_count, rows], cotangent[rows, :])

    zero = jnp.zeros((coarse_count, width), f32)
    cot_all[c] = lax.fori_loop(0, blocks, prepare, zero)
    cot_copies = [
        remote(cot_all.at[c], cot_all.at[c], cot_send.at[d], cot_recv.at[c], (a, peer))
        for d, peer in enumerate(across_peers)
    ]
    for copy in cot_copies:
        copy.start()
    w_joined[...] = dot(w_msg[...], w_second).astype(bf16)

    for load in loads[6:9]:
        load.wait()
    for side, (has_target, device, has_source) in enumerate(sides):

        @pl.when(has_source)
        def _(side=side):
            halo(side, (a, c)).wait_recv()

    def aggregate(b, pooled):
        rows = tile_rows(b)
        gathered = jnp.concatenate([sources[adj_index[k, b]] for k in range(slots)], axis=0)
        weights = jnp.concatenate(
            [
                adj[b, k] * jnp.where(k < adj_count[0, b], 1.0, 0.0).astype(bf16)
                for k in range(slots)
            ],
            axis=1,
        )
        block_sum = dot(weights, gathered).astype(bf16)
        summed[rows, :] = block_sum
        v = pre[rows, :] + dot(block_sum, w_joined[...])
        s = sigmoid(v)
        slope[rows, :] = s * (1.0 + v * (1.0 - s))
        h = features[rows, :].astype(f32) + v * s
        hidden[rows, :] = h
        high, low = split(h)
        pick = picks[0:coarse_count, rows]
        return pooled + dot(pick, high) + dot(pick, low)

    pooled = lax.fori_loop(0, blocks, aggregate, zero)
    pool_all[c] = pooled
    pool_copies = [
        remote(pool_all.at[c], pool_all.at[c], pool_send.at[d], pool_recv.at[c], (a, peer))
        for d, peer in enumerate(across_peers)
    ]
    for copy in pool_copies:
        copy.start()

    def transpose(b, carry):
        summed_t[:, tile_rows(b)] = summed[tile_rows(b), :].T
        return carry

    lax.fori_loop(0, blocks, transpose, 0)
    loads[9].wait()

    for peer in across_peers:
        remote(
            cot_all.at[peer], cot_all.at[peer], cot_send.at[0], cot_recv.at[peer], (a, c)
        ).wait_recv()
        remote(
            pool_all.at[peer], pool_all.at[peer], pool_send.at[0], pool_recv.at[peer], (a, c)
        ).wait_recv()
    pooled, coarse_cot = pool_all[0], cot_all[0]
    for i in range(1, n_across):
        pooled, coarse_cot = pooled + pool_all[i], coarse_cot + cot_all[i]

    coarse_norm, inverse = normalize(pooled)
    coarse = coarse_norm.astype(bf16)
    coarse_pre = dot(coarse, w_coarse[...])
    s = sigmoid(coarse_pre)
    coarse_out = (coarse_pre * s).astype(bf16)
    coarse_delta = (coarse_cot * (s * (1.0 + coarse_pre * (1.0 - s)))).astype(bf16)
    pack[0:coarse_count, :] = coarse
    pack[coarse_count : 2 * coarse_count, :] = coarse_delta

    def send_pack(target):
        return remote(pack, pack_all.at[a], pack_send.at[target - half], pack_recv.at[a], (target, c))

    for target in range(half, n_along):

        @pl.when(a != target)
        def _(target=target):
            send_pack(target).start()

    coarse_back = times_transposed(coarse_delta, w_coarse[...])
    mean_one = jnp.mean(coarse_back, axis=-1, keepdims=True)
    mean_two = jnp.mean(coarse_back * coarse_norm, axis=-1, keepdims=True)
    pooled_delta = inverse * (coarse_back - mean_one - coarse_norm * mean_two)
    delta_parts = jnp.concatenate(split(pooled_delta), axis=0)

    total[...] = jnp.zeros(total.shape, f32)

    def backward(b, carry):
        rows = tile_rows(b, 2)
        spread = transposed_times(picks[:, rows], delta_parts)
        hidden_delta = cotangent[rows, :].astype(f32) + spread
        update_delta = (hidden_delta * slope[rows, :]).astype(bf16)
        total[...] += dot(summed_t[:, rows], update_delta)
        return carry

    lax.fori_loop(0, blocks // 2, backward, 0)

    for i in range(half):
        for j in range(n_across):
            start = (i * n_across + j) * chunk
            part[j, i] = total[start : start + chunk, :].astype(bf16)

    def send_part(i, d, peer):
        return remote(
            part.at[peer, i], part_all.at[c, i], part_send.at[d, i], part_recv.at[c, i], (a, peer)
        )

    for i in reversed(range(half)):
        for d, peer in enumerate(across_peers):
            send_part(i, d, peer).start()

    def update(b, carry):
        rows = tile_rows(b)
        spread = transposed_times(picks[0:coarse_count, rows], coarse_out)
        updated[rows, :] = (hidden[rows, :] + spread).astype(bf16)
        return carry

    lax.fori_loop(0, blocks, update, 0)
    store = pltpu.make_async_copy(updated, updated_hbm, out_sem.at[0])
    store.start()

    def send_second(i):
        return remote(
            second.at[i], second_all.at[a], second_send.at[i], second_recv.at[a], (i, c)
        )

    for i in reversed(range(half)):
        start = pl.multiple_of((i * n_across + c) * chunk, chunk)
        chunk_sum = total[pl.ds(start, chunk), :]
        for peer in across_peers:
            remote(
                part.at[peer, i], part_all.at[peer, i], part_send.at[0, i], part_recv.at[peer, i], (a, c)
            ).wait_recv()
            chunk_sum = chunk_sum + part_all[peer, i].astype(f32)

        @pl.when(a == i)
        def _(chunk_sum=chunk_sum):
            own_chunk[...] = chunk_sum

        @pl.when(a != i)
        def _(chunk_sum=chunk_sum, i=i):
            second[i] = chunk_sum.astype(bf16)
            send_second(i).start()

    @pl.when(a < half)
    def _():
        chunk_sum = own_chunk[...]
        for peer in along_peers:
            remote(
                second.at[0], second_all.at[peer], second_send.at[0], second_recv.at[peer], (a, c)
            ).wait_recv()
            chunk_sum = chunk_sum + second_all[peer].astype(f32)
        high, low = split(chunk_sum)
        both = times_transposed(jnp.concatenate([high, low], axis=0), w_second)
        put_grads(both[0:chunk, :] + both[chunk : 2 * chunk, :])

    @pl.when(a >= half)
    def _():
        pack_all[a] = pack[...]
        for peer in along_peers:
            remote(
                pack, pack_all.at[peer], pack_send.at[0], pack_recv.at[peer], (a, c)
            ).wait_recv()
        rows = n_along * coarse_count
        all_coarse = pack_all[:, 0:coarse_count, :].reshape(rows, width)
        all_delta = pack_all[:, coarse_count : 2 * coarse_count, :].reshape(rows, width)
        coarse_grad[...] = transposed_times(all_coarse, all_delta)
        start = pl.multiple_of(((a - half) * n_across + c) * chunk, chunk)
        put_grads(coarse_grad[pl.ds(start, chunk), :])

    for side, (has_target, device, has_source) in enumerate(sides):

        @pl.when(has_target)
        def _(side=side, device=device):
            halo(side, device).wait_send()

    for copy in cot_copies + pool_copies:
        copy.wait_send()
    for target in range(half, n_along):

        @pl.when(a != target)
        def _(target=target):
            send_pack(target).wait_send()

    for i in range(half):
        for d, peer in enumerate(across_peers):
            send_part(i, d, peer).wait_send()

        @pl.when(a != i)
        def _(i=i):
            send_second(i).wait_send()

    store.wait()


def fused_layer(
    n_along,
    n_across,
    chunk,
    features,
    adj_tiles,
    adj_index,
    adj_count,
    bnd_index,
    pool_index,
    w_msg,
    w_update,
    w_coarse,
    cotangent,
):
    nodes, width = features.shape
    blocks, slots, tile, _ = adj_tiles.shape
    half = n_along // 2
    coarse_count = NC_DEV * n_across
    vmem = pltpu.VMEM
    dma = pltpu.SemaphoreType.DMA
    hbm_spec = pl.BlockSpec(memory_space=pltpu.HBM)
    vmem_spec = pl.BlockSpec(memory_space=pltpu.VMEM)
    any_spec = pl.BlockSpec(memory_space=pl.ANY)
    updated, grads = pl.pallas_call(
        functools.partial(layer_kernel, n_along, n_across),
        name="mesh_layer",
        out_shape=(
            vmem((nodes, width), bf16),
            vmem((chunk * width // 128, 128), f32),
        ),
        in_specs=[hbm_spec] * 10,
        out_specs=(any_spec, vmem_spec),
        scratch_shapes=[
            pltpu.SMEM((slots, blocks), jnp.int32),
            pltpu.SMEM((1, blocks), jnp.int32),
            vmem((1, tile), jnp.int32),
            vmem((1, nodes), jnp.int32),
            vmem((nodes, width), bf16),
            vmem(adj_tiles.shape, bf16),
            vmem(w_msg.shape, bf16),
            vmem(w_update.shape, bf16),
            vmem(w_coarse.shape, bf16),
            vmem((nodes, width), bf16),
            vmem((blocks + 4, tile, width), bf16),
            vmem((tile, width), bf16),
            vmem((width, width), bf16),
            vmem((nodes, width), f32),
            vmem((nodes, width), f32),
            vmem((nodes, width), f32),
            vmem((nodes, width), bf16),
            vmem((width, nodes), bf16),
            vmem((2 * coarse_count, nodes), bf16),
            vmem((nodes, width), bf16),
            vmem((n_across, coarse_count, width), f32),
            vmem((n_across, coarse_count, width), f32),
            vmem((2 * coarse_count, width), bf16),
            vmem((n_along, 2 * coarse_count, width), bf16),
            vmem((width, width), f32),
            vmem((width, width), f32),
            vmem((n_across, half, chunk, width), bf16),
            vmem((n_across, half, chunk, width), bf16),
            vmem((half, chunk, width), bf16),
            vmem((n_along, chunk, width), bf16),
            vmem((chunk, width), f32),
            dma((10,)),
            dma((1,)),
            dma((4,)),
            dma((4,)),
            dma((n_across,)),
            dma((n_across,)),
            dma((n_across,)),
            dma((n_across,)),
            dma((half,)),
            dma((n_along,)),
            dma((n_across, half)),
            dma((n_across, half)),
            dma((half,)),
            dma((n_along,)),
        ],
        compiler_params=pltpu.CompilerParams(
            collective_id=0, has_side_effects=True, vmem_limit_bytes=60 * 2**20
        ),
        cost_estimate=pl.CostEstimate(
            flops=2 * nodes * width * (slots * tile + 5 * width),
            bytes_accessed=4 * 2**20,
            transcendentals=nodes * width,
        ),
    )(
        adj_index.T,
        adj_count.reshape(1, blocks),
        bnd_index.reshape(1, tile),
        pool_index.reshape(1, nodes),
        features,
        adj_tiles,
        w_msg,
        w_update,
        w_coarse,
        cotangent,
    )
    return updated, grads.reshape(-1)


def layer(axes, features, adj_tiles, *others):
    n_along, n_across = axes["along"], axes["across"]
    width = features.shape[1]
    chunk = 2 * width // (n_along * n_across)
    if n_along % 2 == 0 and chunk and chunk % 16 == 0:
        return fused_layer(n_along, n_across, chunk, features, adj_tiles, *others)
    return plain_layer(features, adj_tiles, *others)


def solution(mesh):
    return jax.shard_map(
        functools.partial(layer, dict(mesh.shape)),
        mesh=mesh,
        in_specs=(
            P(("along", "across"), None),
            P(("along", "across"), None, None, None),
            P(("along", "across"), None),
            P(("along", "across")),
            P(("along", "across")),
            P(("along", "across")),
            P(),
            P(),
            P(),
            P(("along", "across"), None),
        ),
        out_specs=(P(("along", "across"), None), P(("along", "across"))),
        check_vma=False,
    )
```

```python
import functools

import jax
import jax.numpy as jnp
from jax import lax
from jax.experimental import pallas as pl
from jax.experimental.pallas import tpu as pltpu
from jax.sharding import PartitionSpec as P

NC_DEV = 4


eps = 1e-05


def extended(block, sides, width):
    for axis, dim in sides:
        count = lax.axis_size(axis)
        forward = [(i, i + 1) for i in range(count - 1)]
        backward = [(target, source) for source, target in forward]
        low = lax.ppermute(
            lax.slice_in_dim(block, block.shape[dim] - width, None, axis=dim), axis, forward
        )
        high = lax.ppermute(lax.slice_in_dim(block, 0, width, axis=dim), axis, backward)
        block = jnp.concatenate([low, block, high], axis=dim)
    return block


def normalize(values):
    center = values - jnp.mean(values, axis=-1, keepdims=True)
    inverse = lax.rsqrt(jnp.mean(center * center, axis=-1, keepdims=True) + eps)
    return (center * inverse, inverse)


def silu_slope(values):
    logistic = jax.nn.sigmoid(values)
    return logistic * (1.0 + values * (1.0 - logistic))


def transposed_times(operand, second, precision=None):
    return lax.dot_general(
        operand,
        second,
        (((0,), (0,)), ((), ())),
        precision=precision,
        preferred_element_type=jnp.float32,
    )


def times_transposed(operand, second):
    return lax.dot_general(
        operand, second, (((1,), (1,)), ((), ())), preferred_element_type=jnp.float32
    )


def coarse_forward(pooled, w_coarse):
    coarse_norm, inverse = normalize(pooled)
    coarse = coarse_norm.astype(jnp.bfloat16)
    coarse_pre = jnp.dot(coarse, w_coarse, preferred_element_type=jnp.float32)
    return (coarse_norm, inverse, coarse, coarse_pre, jax.nn.silu(coarse_pre).astype(jnp.bfloat16))


def coarse_backward(coarse_cot, coarse_norm, inverse, coarse_pre, w_coarse):
    coarse_delta = (coarse_cot * silu_slope(coarse_pre)).astype(jnp.bfloat16)
    coarse_back = times_transposed(coarse_delta, w_coarse)
    mean_one = jnp.mean(coarse_back, axis=-1, keepdims=True)
    mean_two = jnp.mean(coarse_back * coarse_norm, axis=-1, keepdims=True)
    return (coarse_delta, inverse * (coarse_back - mean_one - coarse_norm * mean_two))


def plain_layer(
    features,
    adj_tiles,
    adj_index,
    adj_count,
    bnd_index,
    pool_index,
    w_msg,
    w_update,
    w_coarse,
    cotangent,
):
    feature_count = features.shape[1]
    blocks = adj_tiles.shape[0]
    slot_count = adj_tiles.shape[1]
    tile_rows = adj_tiles.shape[2]
    inputs = features.astype(jnp.float32)
    normed, _ = normalize(inputs)
    scaled = normed.astype(jnp.bfloat16)
    rim_rows = scaled[bnd_index]
    padded = extended(rim_rows[None, None], (("along", 0), ("across", 1)), 1)
    halo_tiles = jnp.stack([padded[0, 1], padded[2, 1], padded[1, 0], padded[1, 2]])
    sources = jnp.concatenate(
        [scaled.reshape(blocks, tile_rows, feature_count), halo_tiles], axis=0
    )
    messages = jnp.dot(
        sources.reshape(-1, feature_count), w_msg, preferred_element_type=jnp.float32
    )
    messages = messages.astype(jnp.bfloat16).reshape(sources.shape)
    live_slots = jnp.arange(slot_count)[None, :] < adj_count[:, None]
    masked_tiles = jnp.where(live_slots[:, :, None, None], adj_tiles, jnp.zeros((), jnp.bfloat16))
    aggregated = jnp.einsum(
        "bkij,bkjh->bih", masked_tiles, messages[adj_index], preferred_element_type=jnp.float32
    )
    aggregated = aggregated.astype(jnp.bfloat16).reshape(-1, feature_count)
    summed_scaled = jnp.einsum(
        "bkij,bkjh->bih", masked_tiles, sources[adj_index], preferred_element_type=jnp.float32
    )
    summed_scaled = summed_scaled.astype(jnp.bfloat16).reshape(-1, feature_count)
    w_first = w_update[:feature_count]
    w_second = w_update[feature_count:]
    update_pre = jnp.dot(scaled, w_first, preferred_element_type=jnp.float32) + jnp.dot(
        aggregated, w_second, preferred_element_type=jnp.float32
    )
    hidden_one = inputs + jax.nn.silu(update_pre)
    coarse_count = NC_DEV * lax.axis_size("across")
    assign_float = (pool_index[:, None] == jnp.arange(coarse_count)[None, :]).astype(jnp.float32)
    assign_bits = assign_float.astype(jnp.bfloat16)
    pooled_part = transposed_times(assign_float, hidden_one, lax.Precision.HIGHEST)
    cot_part = transposed_times(assign_bits, cotangent)
    pooled, coarse_cot = lax.psum((pooled_part, cot_part), "across")
    coarse_norm, inverse, coarse, coarse_pre, coarse_out = coarse_forward(pooled, w_coarse)
    hidden_two = hidden_one + jnp.dot(assign_bits, coarse_out, preferred_element_type=jnp.float32)
    coarse_delta, pooled_delta = coarse_backward(
        coarse_cot, coarse_norm, inverse, coarse_pre, w_coarse
    )
    start = lax.axis_index("across") * NC_DEV
    own_coarse = lax.dynamic_slice_in_dim(coarse, start, NC_DEV, 0)
    own_coarse_delta = lax.dynamic_slice_in_dim(coarse_delta, start, NC_DEV, 0)
    coarse_grad = transposed_times(own_coarse, own_coarse_delta)
    hidden_delta = cotangent.astype(jnp.float32) + jnp.dot(
        assign_float,
        pooled_delta,
        precision=lax.Precision.HIGHEST,
        preferred_element_type=jnp.float32,
    )
    update_delta = (hidden_delta * silu_slope(update_pre)).astype(jnp.bfloat16)
    aggregated_delta = times_transposed(update_delta, w_second).astype(jnp.bfloat16)
    message_grad = transposed_times(summed_scaled, aggregated_delta)
    grad_terms = jnp.concatenate([message_grad.reshape(-1), coarse_grad.reshape(-1)])
    partial_grads = lax.psum_scatter(grad_terms, "along", scatter_dimension=0, tiled=True)
    weight_grads = lax.psum_scatter(partial_grads, "across", scatter_dimension=0, tiled=True)
    return (hidden_two.astype(jnp.bfloat16), weight_grads)


MESH = pl.DeviceIdType.MESH
f32 = jnp.float32
bf16 = jnp.bfloat16


def split(values):
    high = values.astype(bf16)
    return high, (values - high.astype(f32)).astype(bf16)


def dot(first, second):
    return jnp.dot(first, second, preferred_element_type=f32)


def sigmoid(values):
    return 0.5 * jnp.tanh(0.5 * values) + 0.5


def layer_kernel(
    n_along,
    n_across,
    index_hbm,
    count_hbm,
    bnd_hbm,
    pool_hbm,
    features_hbm,
    adj_hbm,
    w_msg_hbm,
    w_update_hbm,
    w_coarse_hbm,
    cotangent_hbm,
    updated_hbm,
    grads,
    adj_index,
    adj_count,
    bnd_row,
    pool_row,
    features,
    adj,
    w_msg,
    w_update,
    w_coarse,
    cotangent,
    sources,
    rim,
    w_joined,
    pre,
    hidden,
    slope,
    summed,
    summed_t,
    update_delta,
    hidden_parts,
    pick_rows,
    updated,
    pool_all,
    cot_all,
    pack,
    pack_all,
    coarse_grad,
    total,
    part,
    part_all,
    second,
    second_all,
    own_chunk,
    in_sem,
    out_sem,
    halo_send,
    halo_recv,
    pool_send,
    pool_recv,
    cot_send,
    cot_recv,
    pack_send,
    pack_recv,
    part_send,
    part_recv,
    second_send,
    second_recv,
):
    a = lax.axis_index("along")
    c = lax.axis_index("across")
    half = n_along // 2
    nodes, width = features.shape
    blocks, slots, tile, _ = adj.shape
    coarse_count = NC_DEV * n_across
    chunk = own_chunk.shape[0]

    def put_grads(values):
        lanes = grads.shape[1]
        parts = width // lanes
        for i in range(parts):
            grads[pl.ds(i, chunk, stride=parts), :] = values[:, i * lanes : (i + 1) * lanes]

    loads = [
        pltpu.make_async_copy(source, target, in_sem.at[i])
        for i, (source, target) in enumerate(
            (
                (features_hbm, features),
                (bnd_hbm, bnd_row),
                (pool_hbm, pool_row),
                (cotangent_hbm, cotangent),
                (w_update_hbm, w_update),
                (w_msg_hbm, w_msg),
                (index_hbm, adj_index),
                (count_hbm, adj_count),
                (adj_hbm, adj),
                (w_coarse_hbm, w_coarse),
            )
        )
    ]
    for load in loads:
        load.start()

    barrier = pltpu.get_barrier_semaphore()
    across_peers = [lax.rem(c + d, n_across) for d in range(1, n_across)]
    z, x = lax.div(a, 2), lax.rem(a, 2)
    layers, owners = n_along // 2, half // 2
    group = 2 * n_across
    place = x * n_across + c
    places = [lax.rem(place + d, group) for d in range(1, group)]
    group_peers = [(2 * z + lax.div(q, n_across), lax.rem(q, n_across)) for q in places]
    layer_peers = [lax.rem(z + d, layers) for d in range(1, layers)]
    along_peers = [lax.rem(a + d, n_along) for d in range(1, n_along)]
    greeted = group_peers + [(2 * peer + i, c) for peer in layer_peers for i in range(2)]
    for device in greeted:
        pl.semaphore_signal(barrier, inc=1, device_id=device, device_id_type=MESH)

    def remote(source, target, send, recv, device):
        return pltpu.make_async_remote_copy(
            src_ref=source,
            dst_ref=target,
            send_sem=send,
            recv_sem=recv,
            device_id=device,
            device_id_type=MESH,
        )

    loads[1].wait()
    bnd_column = jnp.broadcast_to(bnd_row[...].astype(f32), (tile, tile)).T[:, 0:1]
    lanes = lax.broadcasted_iota(jnp.int32, (tile, nodes), 1)
    rim_pick = (lanes == bnd_column.astype(jnp.int32)).astype(f32).astype(bf16)
    loads[0].wait()
    rim[...] = normalize(dot(rim_pick, features[...]))[0].astype(bf16)

    pl.semaphore_wait(barrier, len(greeted))

    sides = (
        (a < n_along - 1, (a + 1, c), a > 0),
        (a > 0, (a - 1, c), a < n_along - 1),
        (c < n_across - 1, (a, c + 1), c > 0),
        (c > 0, (a, c - 1), c < n_across - 1),
    )

    def halo(side, device):
        return remote(
            rim, sources.at[blocks + side], halo_send.at[side], halo_recv.at[side], device
        )

    for side, (has_target, device, has_source) in enumerate(sides):

        @pl.when(has_target)
        def _(side=side, device=device):
            halo(side, device).start()

        @pl.when(jnp.logical_not(has_source))
        def _(side=side):
            sources[blocks + side] = jnp.zeros((tile, width), bf16)

    for b in range(blocks):
        block = features[b * tile : (b + 1) * tile, :].astype(f32)
        sources[b] = normalize(block)[0].astype(bf16)

    loads[2].wait()
    pool_pick = (
        lax.broadcasted_iota(jnp.int32, (coarse_count, nodes), 0) == pool_row[...]
    ).astype(f32).astype(bf16)
    pick_rows[...] = jnp.concatenate([pool_pick, pool_pick], axis=0).astype(f32).T.astype(bf16)
    loads[3].wait()
    cot_all[c] = dot(pool_pick, cotangent[...])
    cot_copies = [
        remote(cot_all.at[c], cot_all.at[c], cot_send.at[d], cot_recv.at[c], (a, peer))
        for d, peer in enumerate(across_peers)
    ]
    for copy in cot_copies:
        copy.start()

    loads[4].wait()
    loads[5].wait()
    w_first = w_update[0:width, :]
    w_second = w_update[width : 2 * width, :]
    w_joined[...] = dot(w_msg[...], w_second).astype(bf16)
    pre[...] = dot(sources[0:blocks].reshape(nodes, width), w_first)

    for load in loads[6:9]:
        load.wait()
    for side, (has_target, device, has_source) in enumerate(sides):

        @pl.when(has_source)
        def _(side=side):
            halo(side, (a, c)).wait_recv()

    for b in range(blocks):
        gathered = jnp.concatenate([sources[adj_index[k, b]] for k in range(slots)], axis=0)
        weights = jnp.concatenate(
            [
                adj[b, k] * jnp.where(k < adj_count[0, b], 1.0, 0.0).astype(bf16)
                for k in range(slots)
            ],
            axis=1,
        )
        summed[b * tile : (b + 1) * tile, :] = dot(weights, gathered).astype(bf16)
    for b in range(0, blocks, 2):
        rows = slice(b * tile, (b + 2) * tile)
        v = pre[rows, :] + dot(summed[rows, :], w_joined[...])
        s = sigmoid(v)
        slope[rows, :] = s * (1.0 + v * (1.0 - s))
        h = features[rows, :].astype(f32) + v * s
        hidden[rows, :] = h
        hidden_parts[0, rows, :], hidden_parts[1, rows, :] = split(h)
    pooled = dot(pool_pick, hidden_parts[0]) + dot(pool_pick, hidden_parts[1])
    pool_all[c] = pooled
    pool_copies = [
        remote(pool_all.at[c], pool_all.at[c], pool_send.at[d], pool_recv.at[c], (a, peer))
        for d, peer in enumerate(across_peers)
    ]
    for copy in pool_copies:
        copy.start()

    for b in range(blocks):
        rows = slice(b * tile, (b + 1) * tile)
        summed_t[:, rows] = summed[rows, :].T
    loads[9].wait()

    for peer in across_peers:
        remote(
            cot_all.at[peer], cot_all.at[peer], cot_send.at[0], cot_recv.at[peer], (a, c)
        ).wait_recv()
        remote(
            pool_all.at[peer], pool_all.at[peer], pool_send.at[0], pool_recv.at[peer], (a, c)
        ).wait_recv()
    pooled, coarse_cot = pool_all[0], cot_all[0]
    for i in range(1, n_across):
        pooled, coarse_cot = pooled + pool_all[i], coarse_cot + cot_all[i]

    coarse_norm, inverse = normalize(pooled)
    coarse = coarse_norm.astype(bf16)
    coarse_pre = dot(coarse, w_coarse[...])
    s = sigmoid(coarse_pre)
    coarse_out = (coarse_pre * s).astype(bf16)
    coarse_delta = (coarse_cot * (s * (1.0 + coarse_pre * (1.0 - s)))).astype(bf16)
    pack[0:coarse_count, :] = coarse
    pack[coarse_count : 2 * coarse_count, :] = coarse_delta

    def send_pack(target):
        return remote(pack, pack_all.at[a], pack_send.at[target - half], pack_recv.at[a], (target, c))

    for target in range(half, n_along):

        @pl.when(a != target)
        def _(target=target):
            send_pack(target).start()

    coarse_back = times_transposed(coarse_delta, w_coarse[...])
    mean_one = jnp.mean(coarse_back, axis=-1, keepdims=True)
    mean_two = jnp.mean(coarse_back * coarse_norm, axis=-1, keepdims=True)
    pooled_delta = inverse * (coarse_back - mean_one - coarse_norm * mean_two)
    delta_parts = jnp.concatenate(split(pooled_delta), axis=0)
    for b in range(0, blocks, 2):
        rows = slice(b * tile, (b + 2) * tile)
        hidden_delta = cotangent[rows, :].astype(f32) + dot(pick_rows[rows, :], delta_parts)
        update_delta[rows, :] = (hidden_delta * slope[rows, :]).astype(bf16)
    total[...] = dot(summed_t[...], update_delta[...])

    for q in range(group):
        for i in range(owners):
            start = ((2 * i + q // n_across) * n_across + q % n_across) * chunk
            part[q, i] = total[start : start + chunk, :].astype(bf16)

    def send_part(i, d):
        return remote(
            part.at[places[d], i],
            part_all.at[place, i],
            part_send.at[d, i],
            part_recv.at[place, i],
            group_peers[d],
        )

    for i in range(owners):
        for d in range(group - 1):
            send_part(i, d).start()

    for b in range(blocks):
        rows = slice(b * tile, (b + 1) * tile)
        spread = dot(pick_rows[rows, 0:coarse_count], coarse_out)
        updated[rows, :] = (hidden[rows, :] + spread).astype(bf16)
    store = pltpu.make_async_copy(updated, updated_hbm, out_sem.at[0])
    store.start()

    def send_second(i):
        return remote(
            second.at[i], second_all.at[z], second_send.at[i], second_recv.at[z], (2 * i + x, c)
        )

    for i in range(owners):
        start = pl.multiple_of(((2 * i + x) * n_across + c) * chunk, chunk)
        chunk_sum = total[pl.ds(start, chunk), :]
        for q in places:
            remote(
                part.at[q, i], part_all.at[q, i], part_send.at[0, i], part_recv.at[q, i], (a, c)
            ).wait_recv()
            chunk_sum = chunk_sum + part_all[q, i].astype(f32)

        @pl.when(z == i)
        def _(chunk_sum=chunk_sum):
            own_chunk[...] = chunk_sum

        @pl.when(z != i)
        def _(chunk_sum=chunk_sum, i=i):
            second[i] = chunk_sum.astype(bf16)
            send_second(i).start()

    @pl.when(a < half)
    def _():
        chunk_sum = own_chunk[...]
        for peer in layer_peers:
            remote(
                second.at[0], second_all.at[peer], second_send.at[0], second_recv.at[peer], (a, c)
            ).wait_recv()
            chunk_sum = chunk_sum + second_all[peer].astype(f32)
        high, low = split(chunk_sum)
        both = times_transposed(jnp.concatenate([high, low], axis=0), w_second)
        put_grads(both[0:chunk, :] + both[chunk : 2 * chunk, :])

    @pl.when(a >= half)
    def _():
        pack_all[a] = pack[...]
        for peer in along_peers:
            remote(
                pack, pack_all.at[peer], pack_send.at[0], pack_recv.at[peer], (a, c)
            ).wait_recv()
        rows = n_along * coarse_count
        all_coarse = pack_all[:, 0:coarse_count, :].reshape(rows, width)
        all_delta = pack_all[:, coarse_count : 2 * coarse_count, :].reshape(rows, width)
        coarse_grad[...] = transposed_times(all_coarse, all_delta)
        start = pl.multiple_of(((a - half) * n_across + c) * chunk, chunk)
        put_grads(coarse_grad[pl.ds(start, chunk), :])

    for side, (has_target, device, has_source) in enumerate(sides):

        @pl.when(has_target)
        def _(side=side, device=device):
            halo(side, device).wait_send()

    for copy in cot_copies + pool_copies:
        copy.wait_send()
    for target in range(half, n_along):

        @pl.when(a != target)
        def _(target=target):
            send_pack(target).wait_send()

    for i in range(owners):
        for d in range(group - 1):
            send_part(i, d).wait_send()

        @pl.when(z != i)
        def _(i=i):
            send_second(i).wait_send()

    store.wait()


def fused_layer(
    n_along,
    n_across,
    chunk,
    features,
    adj_tiles,
    adj_index,
    adj_count,
    bnd_index,
    pool_index,
    w_msg,
    w_update,
    w_coarse,
    cotangent,
):
    nodes, width = features.shape
    blocks, slots, tile, _ = adj_tiles.shape
    half = n_along // 2
    coarse_count = NC_DEV * n_across
    vmem = pltpu.VMEM
    dma = pltpu.SemaphoreType.DMA
    hbm_spec = pl.BlockSpec(memory_space=pltpu.HBM)
    vmem_spec = pl.BlockSpec(memory_space=pltpu.VMEM)
    any_spec = pl.BlockSpec(memory_space=pl.ANY)
    updated, grads = pl.pallas_call(
        functools.partial(layer_kernel, n_along, n_across),
        name="mesh_layer",
        out_shape=(
            vmem((nodes, width), bf16),
            vmem((chunk * width // 128, 128), f32),
        ),
        in_specs=[hbm_spec] * 10,
        out_specs=(any_spec, vmem_spec),
        scratch_shapes=[
            pltpu.SMEM((slots, blocks), jnp.int32),
            pltpu.SMEM((1, blocks), jnp.int32),
            vmem((1, tile), jnp.int32),
            vmem((1, nodes), jnp.int32),
            vmem((nodes, width), bf16),
            vmem(adj_tiles.shape, bf16),
            vmem(w_msg.shape, bf16),
            vmem(w_update.shape, bf16),
            vmem(w_coarse.shape, bf16),
            vmem((nodes, width), bf16),
            vmem((blocks + 4, tile, width), bf16),
            vmem((tile, width), bf16),
            vmem((width, width), bf16),
            vmem((nodes, width), f32),
            vmem((nodes, width), f32),
            vmem((nodes, width), f32),
            vmem((nodes, width), bf16),
            vmem((width, nodes), bf16),
            vmem((nodes, width), bf16),
            vmem((2, nodes, width), bf16),
            vmem((nodes, 2 * coarse_count), bf16),
            vmem((nodes, width), bf16),
            vmem((n_across, coarse_count, width), f32),
            vmem((n_across, coarse_count, width), f32),
            vmem((2 * coarse_count, width), bf16),
            vmem((n_along, 2 * coarse_count, width), bf16),
            vmem((width, width), f32),
            vmem((width, width), f32),
            vmem((2 * n_across, half // 2, chunk, width), bf16),
            vmem((2 * n_across, half // 2, chunk, width), bf16),
            vmem((half // 2, chunk, width), bf16),
            vmem((n_along // 2, chunk, width), bf16),
            vmem((chunk, width), f32),
            dma((10,)),
            dma((1,)),
            dma((4,)),
            dma((4,)),
            dma((n_across,)),
            dma((n_across,)),
            dma((n_across,)),
            dma((n_across,)),
            dma((half,)),
            dma((n_along,)),
            dma((2 * n_across, half // 2)),
            dma((2 * n_across, half // 2)),
            dma((half // 2,)),
            dma((n_along // 2,)),
        ],
        compiler_params=pltpu.CompilerParams(
            collective_id=0, has_side_effects=True, vmem_limit_bytes=60 * 2**20
        ),
        cost_estimate=pl.CostEstimate(
            flops=2 * nodes * width * (slots * tile + 5 * width),
            bytes_accessed=4 * 2**20,
            transcendentals=nodes * width,
        ),
    )(
        adj_index.T,
        adj_count.reshape(1, blocks),
        bnd_index.reshape(1, tile),
        pool_index.reshape(1, nodes),
        features,
        adj_tiles,
        w_msg,
        w_update,
        w_coarse,
        cotangent,
    )
    return updated, grads.reshape(-1)


def layer(axes, features, adj_tiles, *others):
    n_along, n_across = axes["along"], axes["across"]
    width = features.shape[1]
    chunk = 2 * width // (n_along * n_across)
    if n_along % 4 == 0 and chunk and chunk % 16 == 0:
        return fused_layer(n_along, n_across, chunk, features, adj_tiles, *others)
    return plain_layer(features, adj_tiles, *others)


def solution(mesh):
    return jax.shard_map(
        functools.partial(layer, dict(mesh.shape)),
        mesh=mesh,
        in_specs=(
            P(("along", "across"), None),
            P(("along", "across"), None, None, None),
            P(("along", "across"), None),
            P(("along", "across")),
            P(("along", "across")),
            P(("along", "across")),
            P(),
            P(),
            P(),
            P(("along", "across"), None),
        ),
        out_specs=(P(("along", "across"), None), P(("along", "across"))),
        check_vma=False,
    )
```

```python
import functools

import jax
import jax.numpy as jnp
from jax import lax
from jax.experimental import pallas as pl
from jax.experimental.pallas import tpu as pltpu
from jax.sharding import PartitionSpec as P

NC_DEV = 4


eps = 1e-05


def extended(block, sides, width):
    for axis, dim in sides:
        count = lax.axis_size(axis)
        forward = [(i, i + 1) for i in range(count - 1)]
        backward = [(target, source) for source, target in forward]
        low = lax.ppermute(
            lax.slice_in_dim(block, block.shape[dim] - width, None, axis=dim), axis, forward
        )
        high = lax.ppermute(lax.slice_in_dim(block, 0, width, axis=dim), axis, backward)
        block = jnp.concatenate([low, block, high], axis=dim)
    return block


def normalize(values):
    center = values - jnp.mean(values, axis=-1, keepdims=True)
    inverse = lax.rsqrt(jnp.mean(center * center, axis=-1, keepdims=True) + eps)
    return (center * inverse, inverse)


def silu_slope(values):
    logistic = jax.nn.sigmoid(values)
    return logistic * (1.0 + values * (1.0 - logistic))


def transposed_times(operand, second, precision=None):
    return lax.dot_general(
        operand,
        second,
        (((0,), (0,)), ((), ())),
        precision=precision,
        preferred_element_type=jnp.float32,
    )


def times_transposed(operand, second):
    return lax.dot_general(
        operand, second, (((1,), (1,)), ((), ())), preferred_element_type=jnp.float32
    )


def coarse_forward(pooled, w_coarse):
    coarse_norm, inverse = normalize(pooled)
    coarse = coarse_norm.astype(jnp.bfloat16)
    coarse_pre = jnp.dot(coarse, w_coarse, preferred_element_type=jnp.float32)
    return (coarse_norm, inverse, coarse, coarse_pre, jax.nn.silu(coarse_pre).astype(jnp.bfloat16))


def coarse_backward(coarse_cot, coarse_norm, inverse, coarse_pre, w_coarse):
    coarse_delta = (coarse_cot * silu_slope(coarse_pre)).astype(jnp.bfloat16)
    coarse_back = times_transposed(coarse_delta, w_coarse)
    mean_one = jnp.mean(coarse_back, axis=-1, keepdims=True)
    mean_two = jnp.mean(coarse_back * coarse_norm, axis=-1, keepdims=True)
    return (coarse_delta, inverse * (coarse_back - mean_one - coarse_norm * mean_two))


def plain_layer(
    features,
    adj_tiles,
    adj_index,
    adj_count,
    bnd_index,
    pool_index,
    w_msg,
    w_update,
    w_coarse,
    cotangent,
):
    feature_count = features.shape[1]
    blocks = adj_tiles.shape[0]
    slot_count = adj_tiles.shape[1]
    tile_rows = adj_tiles.shape[2]
    inputs = features.astype(jnp.float32)
    normed, _ = normalize(inputs)
    scaled = normed.astype(jnp.bfloat16)
    rim_rows = scaled[bnd_index]
    padded = extended(rim_rows[None, None], (("along", 0), ("across", 1)), 1)
    halo_tiles = jnp.stack([padded[0, 1], padded[2, 1], padded[1, 0], padded[1, 2]])
    sources = jnp.concatenate(
        [scaled.reshape(blocks, tile_rows, feature_count), halo_tiles], axis=0
    )
    messages = jnp.dot(
        sources.reshape(-1, feature_count), w_msg, preferred_element_type=jnp.float32
    )
    messages = messages.astype(jnp.bfloat16).reshape(sources.shape)
    live_slots = jnp.arange(slot_count)[None, :] < adj_count[:, None]
    masked_tiles = jnp.where(live_slots[:, :, None, None], adj_tiles, jnp.zeros((), jnp.bfloat16))
    aggregated = jnp.einsum(
        "bkij,bkjh->bih", masked_tiles, messages[adj_index], preferred_element_type=jnp.float32
    )
    aggregated = aggregated.astype(jnp.bfloat16).reshape(-1, feature_count)
    summed_scaled = jnp.einsum(
        "bkij,bkjh->bih", masked_tiles, sources[adj_index], preferred_element_type=jnp.float32
    )
    summed_scaled = summed_scaled.astype(jnp.bfloat16).reshape(-1, feature_count)
    w_first = w_update[:feature_count]
    w_second = w_update[feature_count:]
    update_pre = jnp.dot(scaled, w_first, preferred_element_type=jnp.float32) + jnp.dot(
        aggregated, w_second, preferred_element_type=jnp.float32
    )
    hidden_one = inputs + jax.nn.silu(update_pre)
    coarse_count = NC_DEV * lax.axis_size("across")
    assign_float = (pool_index[:, None] == jnp.arange(coarse_count)[None, :]).astype(jnp.float32)
    assign_bits = assign_float.astype(jnp.bfloat16)
    pooled_part = transposed_times(assign_float, hidden_one, lax.Precision.HIGHEST)
    cot_part = transposed_times(assign_bits, cotangent)
    pooled, coarse_cot = lax.psum((pooled_part, cot_part), "across")
    coarse_norm, inverse, coarse, coarse_pre, coarse_out = coarse_forward(pooled, w_coarse)
    hidden_two = hidden_one + jnp.dot(assign_bits, coarse_out, preferred_element_type=jnp.float32)
    coarse_delta, pooled_delta = coarse_backward(
        coarse_cot, coarse_norm, inverse, coarse_pre, w_coarse
    )
    start = lax.axis_index("across") * NC_DEV
    own_coarse = lax.dynamic_slice_in_dim(coarse, start, NC_DEV, 0)
    own_coarse_delta = lax.dynamic_slice_in_dim(coarse_delta, start, NC_DEV, 0)
    coarse_grad = transposed_times(own_coarse, own_coarse_delta)
    hidden_delta = cotangent.astype(jnp.float32) + jnp.dot(
        assign_float,
        pooled_delta,
        precision=lax.Precision.HIGHEST,
        preferred_element_type=jnp.float32,
    )
    update_delta = (hidden_delta * silu_slope(update_pre)).astype(jnp.bfloat16)
    aggregated_delta = times_transposed(update_delta, w_second).astype(jnp.bfloat16)
    message_grad = transposed_times(summed_scaled, aggregated_delta)
    grad_terms = jnp.concatenate([message_grad.reshape(-1), coarse_grad.reshape(-1)])
    partial_grads = lax.psum_scatter(grad_terms, "along", scatter_dimension=0, tiled=True)
    weight_grads = lax.psum_scatter(partial_grads, "across", scatter_dimension=0, tiled=True)
    return (hidden_two.astype(jnp.bfloat16), weight_grads)


MESH = pl.DeviceIdType.MESH
f32 = jnp.float32
bf16 = jnp.bfloat16


def split(values):
    high = values.astype(bf16)
    return high, (values - high.astype(f32)).astype(bf16)


def dot(first, second):
    return jnp.dot(first, second, preferred_element_type=f32)


def sigmoid(values):
    return 0.5 * jnp.tanh(0.5 * values) + 0.5


def layer_kernel(
    n_along,
    n_across,
    index_hbm,
    count_hbm,
    bnd_hbm,
    pool_hbm,
    features_hbm,
    adj_hbm,
    w_msg_hbm,
    w_update_hbm,
    w_coarse_hbm,
    cotangent_hbm,
    updated_hbm,
    grads,
    adj_index,
    adj_count,
    bnd_row,
    pool_row,
    features,
    adj,
    w_msg,
    w_update,
    w_coarse,
    cotangent,
    sources,
    rim,
    w_joined,
    pre,
    hidden,
    slope,
    summed,
    summed_t,
    update_delta,
    hidden_parts,
    pick_rows,
    updated,
    pool_all,
    cot_all,
    pack,
    pack_all,
    coarse_grad,
    total,
    part,
    part_all,
    second,
    second_all,
    own_chunk,
    in_sem,
    out_sem,
    halo_send,
    halo_recv,
    pool_send,
    pool_recv,
    cot_send,
    cot_recv,
    pack_send,
    pack_recv,
    part_send,
    part_recv,
    second_send,
    second_recv,
):
    a = lax.axis_index("along")
    c = lax.axis_index("across")
    half = n_along // 2
    nodes, width = features.shape
    blocks, slots, tile, _ = adj.shape
    coarse_count = NC_DEV * n_across
    chunk = own_chunk.shape[0]

    def put_grads(values):
        lanes = grads.shape[1]
        parts = width // lanes
        for i in range(parts):
            grads[pl.ds(i, chunk, stride=parts), :] = values[:, i * lanes : (i + 1) * lanes]

    loads = [
        pltpu.make_async_copy(source, target, in_sem.at[i])
        for i, (source, target) in enumerate(
            (
                (features_hbm, features),
                (bnd_hbm, bnd_row),
                (pool_hbm, pool_row),
                (cotangent_hbm, cotangent),
                (w_update_hbm, w_update),
                (w_msg_hbm, w_msg),
                (index_hbm, adj_index),
                (count_hbm, adj_count),
                (adj_hbm, adj),
                (w_coarse_hbm, w_coarse),
            )
        )
    ]
    for load in loads[0:2]:
        load.start()

    barrier = pltpu.get_barrier_semaphore()
    across_peers = [lax.rem(c + d, n_across) for d in range(1, n_across)]
    z, x = lax.div(a, 2), lax.rem(a, 2)
    layers, owners = n_along // 2, half // 2
    group = 2 * n_across
    place = x * n_across + c
    places = [lax.rem(place + d, group) for d in range(1, group)]
    group_peers = [(2 * z + lax.div(q, n_across), lax.rem(q, n_across)) for q in places]
    layer_peers = [lax.rem(z + d, layers) for d in range(1, layers)]
    along_peers = [lax.rem(a + d, n_along) for d in range(1, n_along)]
    greeted = group_peers + [(2 * peer + i, c) for peer in layer_peers for i in range(2)]
    for device in greeted:
        pl.semaphore_signal(barrier, inc=1, device_id=device, device_id_type=MESH)
    for load in loads[2:]:
        load.start()

    def remote(source, target, send, recv, device):
        return pltpu.make_async_remote_copy(
            src_ref=source,
            dst_ref=target,
            send_sem=send,
            recv_sem=recv,
            device_id=device,
            device_id_type=MESH,
        )

    loads[1].wait()
    bnd_column = jnp.broadcast_to(bnd_row[...].astype(f32), (tile, tile)).T[:, 0:1]
    lanes = lax.broadcasted_iota(jnp.int32, (tile, nodes), 1)
    rim_pick = (lanes == bnd_column.astype(jnp.int32)).astype(f32).astype(bf16)
    loads[0].wait()
    rim[...] = normalize(dot(rim_pick, features[...]))[0].astype(bf16)

    pl.semaphore_wait(barrier, len(greeted))

    sides = (
        (a < n_along - 1, (a + 1, c), a > 0),
        (a > 0, (a - 1, c), a < n_along - 1),
        (c < n_across - 1, (a, c + 1), c > 0),
        (c > 0, (a, c - 1), c < n_across - 1),
    )

    def halo(side, device):
        return remote(
            rim, sources.at[blocks + side], halo_send.at[side], halo_recv.at[side], device
        )

    for side, (has_target, device, has_source) in enumerate(sides):

        @pl.when(has_target)
        def _(side=side, device=device):
            halo(side, device).start()

        @pl.when(jnp.logical_not(has_source))
        def _(side=side):
            sources[blocks + side] = jnp.zeros((tile, width), bf16)

    for b in range(blocks):
        block = features[b * tile : (b + 1) * tile, :].astype(f32)
        sources[b] = normalize(block)[0].astype(bf16)

    loads[2].wait()
    pool_pick = (
        lax.broadcasted_iota(jnp.int32, (coarse_count, nodes), 0) == pool_row[...]
    ).astype(f32).astype(bf16)
    loads[4].wait()
    loads[5].wait()
    w_first = w_update[0:width, :]
    w_second = w_update[width : 2 * width, :]
    w_joined[...] = dot(w_msg[...], w_second).astype(bf16)
    pre[...] = dot(sources[0:blocks].reshape(nodes, width), w_first)

    for load in loads[6:9]:
        load.wait()
    for side, (has_target, device, has_source) in enumerate(sides):

        @pl.when(has_source)
        def _(side=side):
            halo(side, (a, c)).wait_recv()

    for b in range(blocks):
        gathered = jnp.concatenate([sources[adj_index[k, b]] for k in range(slots)], axis=0)
        weights = jnp.concatenate(
            [
                adj[b, k] * jnp.where(k < adj_count[0, b], 1.0, 0.0).astype(bf16)
                for k in range(slots)
            ],
            axis=1,
        )
        summed[b * tile : (b + 1) * tile, :] = dot(weights, gathered).astype(bf16)
    for b in range(0, blocks, 2):
        rows = slice(b * tile, (b + 2) * tile)
        v = pre[rows, :] + dot(summed[rows, :], w_joined[...])
        s = sigmoid(v)
        slope[rows, :] = s * (1.0 + v * (1.0 - s))
        h = features[rows, :].astype(f32) + v * s
        hidden[rows, :] = h
        hidden_parts[0, rows, :], hidden_parts[1, rows, :] = split(h)
    pooled = dot(pool_pick, hidden_parts[0]) + dot(pool_pick, hidden_parts[1])
    pool_all[c] = pooled
    pool_copies = [
        remote(pool_all.at[c], pool_all.at[c], pool_send.at[d], pool_recv.at[c], (a, peer))
        for d, peer in enumerate(across_peers)
    ]
    for copy in pool_copies:
        copy.start()

    loads[3].wait()
    cot_all[c] = dot(pool_pick, cotangent[...])
    cot_copies = [
        remote(cot_all.at[c], cot_all.at[c], cot_send.at[d], cot_recv.at[c], (a, peer))
        for d, peer in enumerate(across_peers)
    ]
    for copy in cot_copies:
        copy.start()

    pick_rows[...] = jnp.concatenate([pool_pick, pool_pick], axis=0).astype(f32).T.astype(bf16)
    for b in range(blocks):
        rows = slice(b * tile, (b + 1) * tile)
        summed_t[:, rows] = summed[rows, :].T
    loads[9].wait()

    for peer in across_peers:
        remote(
            pool_all.at[peer], pool_all.at[peer], pool_send.at[0], pool_recv.at[peer], (a, c)
        ).wait_recv()
    pooled = pool_all[0]
    for i in range(1, n_across):
        pooled = pooled + pool_all[i]

    coarse_norm, inverse = normalize(pooled)
    coarse = coarse_norm.astype(bf16)
    coarse_pre = dot(coarse, w_coarse[...])
    s = sigmoid(coarse_pre)
    coarse_out = (coarse_pre * s).astype(bf16)
    for peer in across_peers:
        remote(
            cot_all.at[peer], cot_all.at[peer], cot_send.at[0], cot_recv.at[peer], (a, c)
        ).wait_recv()
    coarse_cot = cot_all[0]
    for i in range(1, n_across):
        coarse_cot = coarse_cot + cot_all[i]
    coarse_delta = (coarse_cot * (s * (1.0 + coarse_pre * (1.0 - s)))).astype(bf16)
    pack[0:coarse_count, :] = coarse
    pack[coarse_count : 2 * coarse_count, :] = coarse_delta

    def send_pack(target):
        return remote(pack, pack_all.at[a], pack_send.at[target - half], pack_recv.at[a], (target, c))

    for target in range(half, n_along):

        @pl.when(a != target)
        def _(target=target):
            send_pack(target).start()

    coarse_back = times_transposed(coarse_delta, w_coarse[...])
    mean_one = jnp.mean(coarse_back, axis=-1, keepdims=True)
    mean_two = jnp.mean(coarse_back * coarse_norm, axis=-1, keepdims=True)
    pooled_delta = inverse * (coarse_back - mean_one - coarse_norm * mean_two)
    delta_parts = jnp.concatenate(split(pooled_delta), axis=0)
    for b in range(0, blocks, 2):
        rows = slice(b * tile, (b + 2) * tile)
        hidden_delta = cotangent[rows, :].astype(f32) + dot(pick_rows[rows, :], delta_parts)
        update_delta[rows, :] = (hidden_delta * slope[rows, :]).astype(bf16)
    total[...] = dot(summed_t[...], update_delta[...])

    for q in range(group):
        for i in range(owners):
            start = ((2 * i + q // n_across) * n_across + q % n_across) * chunk
            part[q, i] = total[start : start + chunk, :].astype(bf16)

    def send_part(i, d):
        return remote(
            part.at[places[d], i],
            part_all.at[place, i],
            part_send.at[d, i],
            part_recv.at[place, i],
            group_peers[d],
        )

    for i in range(owners):
        for d in range(group - 1):
            send_part(i, d).start()

    for b in range(blocks):
        rows = slice(b * tile, (b + 1) * tile)
        spread = dot(pick_rows[rows, 0:coarse_count], coarse_out)
        updated[rows, :] = (hidden[rows, :] + spread).astype(bf16)
    store = pltpu.make_async_copy(updated, updated_hbm, out_sem.at[0])
    store.start()

    def send_second(i):
        return remote(
            second.at[i], second_all.at[z], second_send.at[i], second_recv.at[z], (2 * i + x, c)
        )

    for i in range(owners):
        start = pl.multiple_of(((2 * i + x) * n_across + c) * chunk, chunk)
        chunk_sum = total[pl.ds(start, chunk), :]
        for q in places:
            remote(
                part.at[q, i], part_all.at[q, i], part_send.at[0, i], part_recv.at[q, i], (a, c)
            ).wait_recv()
            chunk_sum = chunk_sum + part_all[q, i].astype(f32)

        @pl.when(z == i)
        def _(chunk_sum=chunk_sum):
            own_chunk[...] = chunk_sum

        @pl.when(z != i)
        def _(chunk_sum=chunk_sum, i=i):
            second[i] = chunk_sum.astype(bf16)
            send_second(i).start()

    @pl.when(a < half)
    def _():
        chunk_sum = own_chunk[...]
        for peer in layer_peers:
            remote(
                second.at[0], second_all.at[peer], second_send.at[0], second_recv.at[peer], (a, c)
            ).wait_recv()
            chunk_sum = chunk_sum + second_all[peer].astype(f32)
        high, low = split(chunk_sum)
        both = times_transposed(jnp.concatenate([high, low], axis=0), w_second)
        put_grads(both[0:chunk, :] + both[chunk : 2 * chunk, :])

    @pl.when(a >= half)
    def _():
        pack_all[a] = pack[...]
        for peer in along_peers:
            remote(
                pack, pack_all.at[peer], pack_send.at[0], pack_recv.at[peer], (a, c)
            ).wait_recv()
        rows = n_along * coarse_count
        all_coarse = pack_all[:, 0:coarse_count, :].reshape(rows, width)
        all_delta = pack_all[:, coarse_count : 2 * coarse_count, :].reshape(rows, width)
        coarse_grad[...] = transposed_times(all_coarse, all_delta)
        start = pl.multiple_of(((a - half) * n_across + c) * chunk, chunk)
        put_grads(coarse_grad[pl.ds(start, chunk), :])

    for side, (has_target, device, has_source) in enumerate(sides):

        @pl.when(has_target)
        def _(side=side, device=device):
            halo(side, device).wait_send()

    for copy in cot_copies + pool_copies:
        copy.wait_send()
    for target in range(half, n_along):

        @pl.when(a != target)
        def _(target=target):
            send_pack(target).wait_send()

    for i in range(owners):
        for d in range(group - 1):
            send_part(i, d).wait_send()

        @pl.when(z != i)
        def _(i=i):
            send_second(i).wait_send()

    store.wait()


def store_kernel(updated, grads, updated_hbm, grads_hbm, sem):
    copies = [
        pltpu.make_async_copy(updated, updated_hbm, sem.at[0]),
        pltpu.make_async_copy(grads, grads_hbm, sem.at[1]),
    ]
    for copy in copies:
        copy.start()
    for copy in copies:
        copy.wait()


def fused_layer(
    n_along,
    n_across,
    chunk,
    features,
    adj_tiles,
    adj_index,
    adj_count,
    bnd_index,
    pool_index,
    w_msg,
    w_update,
    w_coarse,
    cotangent,
):
    nodes, width = features.shape
    blocks, slots, tile, _ = adj_tiles.shape
    half = n_along // 2
    coarse_count = NC_DEV * n_across
    vmem = pltpu.VMEM
    dma = pltpu.SemaphoreType.DMA
    hbm_spec = pl.BlockSpec(memory_space=pltpu.HBM)
    vmem_spec = pl.BlockSpec(memory_space=pltpu.VMEM)
    any_spec = pl.BlockSpec(memory_space=pl.ANY)
    updated, grads = pl.pallas_call(
        functools.partial(layer_kernel, n_along, n_across),
        name="mesh_layer",
        out_shape=(
            vmem((nodes, width), bf16),
            vmem((chunk * width // 128, 128), f32),
        ),
        in_specs=[hbm_spec] * 10,
        out_specs=(any_spec, vmem_spec),
        scratch_shapes=[
            pltpu.SMEM((slots, blocks), jnp.int32),
            pltpu.SMEM((1, blocks), jnp.int32),
            vmem((1, tile), jnp.int32),
            vmem((1, nodes), jnp.int32),
            vmem((nodes, width), bf16),
            vmem(adj_tiles.shape, bf16),
            vmem(w_msg.shape, bf16),
            vmem(w_update.shape, bf16),
            vmem(w_coarse.shape, bf16),
            vmem((nodes, width), bf16),
            vmem((blocks + 4, tile, width), bf16),
            vmem((tile, width), bf16),
            vmem((width, width), bf16),
            vmem((nodes, width), f32),
            vmem((nodes, width), f32),
            vmem((nodes, width), f32),
            vmem((nodes, width), bf16),
            vmem((width, nodes), bf16),
            vmem((nodes, width), bf16),
            vmem((2, nodes, width), bf16),
            vmem((nodes, 2 * coarse_count), bf16),
            vmem((nodes, width), bf16),
            vmem((n_across, coarse_count, width), f32),
            vmem((n_across, coarse_count, width), f32),
            vmem((2 * coarse_count, width), bf16),
            vmem((n_along, 2 * coarse_count, width), bf16),
            vmem((width, width), f32),
            vmem((width, width), f32),
            vmem((2 * n_across, half // 2, chunk, width), bf16),
            vmem((2 * n_across, half // 2, chunk, width), bf16),
            vmem((half // 2, chunk, width), bf16),
            vmem((n_along // 2, chunk, width), bf16),
            vmem((chunk, width), f32),
            dma((10,)),
            dma((1,)),
            dma((4,)),
            dma((4,)),
            dma((n_across,)),
            dma((n_across,)),
            dma((n_across,)),
            dma((n_across,)),
            dma((half,)),
            dma((n_along,)),
            dma((2 * n_across, half // 2)),
            dma((2 * n_across, half // 2)),
            dma((half // 2,)),
            dma((n_along // 2,)),
        ],
        compiler_params=pltpu.CompilerParams(
            collective_id=0, has_side_effects=True, vmem_limit_bytes=60 * 2**20
        ),
        cost_estimate=pl.CostEstimate(
            flops=2 * nodes * width * (slots * tile + 5 * width),
            bytes_accessed=4 * 2**20,
            transcendentals=nodes * width,
        ),
    )(
        adj_index.T,
        adj_count.reshape(1, blocks),
        bnd_index.reshape(1, tile),
        pool_index.reshape(1, nodes),
        features,
        adj_tiles,
        w_msg,
        w_update,
        w_coarse,
        cotangent,
    )
    updated, grads = pl.pallas_call(
        store_kernel,
        name="store_results",
        out_shape=(
            jax.ShapeDtypeStruct(updated.shape, bf16),
            jax.ShapeDtypeStruct(grads.shape, f32),
        ),
        in_specs=[any_spec] * 2,
        out_specs=(hbm_spec, hbm_spec),
        scratch_shapes=[dma((2,))],
    )(updated, grads)
    return updated, grads.reshape(-1)


def layer(axes, features, adj_tiles, *others):
    n_along, n_across = axes["along"], axes["across"]
    width = features.shape[1]
    chunk = 2 * width // (n_along * n_across)
    if n_along % 4 == 0 and chunk and chunk % 16 == 0:
        return fused_layer(n_along, n_across, chunk, features, adj_tiles, *others)
    return plain_layer(features, adj_tiles, *others)


def solution(mesh):
    return jax.shard_map(
        functools.partial(layer, dict(mesh.shape)),
        mesh=mesh,
        in_specs=(
            P(("along", "across"), None),
            P(("along", "across"), None, None, None),
            P(("along", "across"), None),
            P(("along", "across")),
            P(("along", "across")),
            P(("along", "across")),
            P(),
            P(),
            P(),
            P(("along", "across"), None),
        ),
        out_specs=(P(("along", "across"), None), P(("along", "across"))),
        check_vma=False,
    )
```
